128 devices in a mesh: table: 4 (over y_lo, core), dp: 32 (over z, x, y_hi).
Axes of the slice: x: 4, y: 4 (y_hi: 2, y_lo: 2; y = y_hi * 2 + y_lo), z: 4, core: 2. Of those that a mesh axis runs over, the one named last changes fastest.
Arguments:
- table: float32 [1048576, 256], P(('table', 'dp')), may hold values from -6 to 6
- feature_owner: int32 [16384, 8], P(('table', 'dp')), may hold values from 0 to 127, all different within a row; in each aligned block of 128 rows (0 to 127, 128 to 255, ...) at most 16 rows name the same one
- feature_offset: int32 [16384, 8], P(('table', 'dp')), may hold values from 0 to 8191
- query_in: bfloat16 [256, 1024], replicated, may hold values from -0.375 to 0.375
- query_out: bfloat16 [1024, 256], replicated, may hold values from -0.1875 to 0.1875
- item_in: bfloat16 [256, 1024], replicated, may hold values from -0.375 to 0.375
- item_out: bfloat16 [1024, 256], replicated, may hold values from -0.1875 to 0.1875
Outputs:
- loss: float32 [16384], P(('table', 'dp'))
- table_grad: float32 [1048576, 256], P(('table', 'dp'))
- query_in_grad: float32 [256, 1024], replicated
- query_out_grad: float32 [1024, 256], replicated
- item_in_grad: float32 [256, 1024], replicated
- item_out_grad: float32 [1024, 256], replicated
The draws below stay inside these ranges and needn't reach their ends.
Inputs may be any that keep to these rules, and one draw needn't show every extreme that they name: `feature_owner`: the 8 ids of a pair lie on different devices. Among the rows of one device no device index appears more than 16 times, and 16 is reached.
All inputs are finite; a program needn't handle non-finite values.
Results may differ from the reference program's by a relative error of at most 0.022.
Values may be sent and summed in bfloat16 or wider, within the bound.
A program may use at most 128 MiB of HBM per device.

```python
import math
import jax
import jax.numpy as jnp
import numpy as np
from jax import lax

E = 256
H = 1024
BAG = 4
PAIRS_DEV = 128
ROWS_DEV = 8192
PAIRS = 16384
BATCH = 4096
ROWS = 1048576
CAP = 16
N_TABLE = 4
N_DP = 32


def set_ends(values, key, smallest, top_value):
    longest = values.shape.index(max(values.shape))
    spots = []
    for shift in (0, 1):
        where = [jax.random.randint(jax.random.fold_in(key, axis), (), 0, length) for axis, length in enumerate(values.shape)]
        where[longest] = (where[longest] + shift) % values.shape[longest]
        spots.append(tuple(where))
    return values.at[spots[0]].set(smallest).at[spots[1]].set(top_value)


def block_scale(key, dims, cuts, least, top_value):
    def one(axis_at, shards_of):
        heights = jax.random.uniform(jax.random.fold_in(jax.random.fold_in(key, 6), axis_at), (shards_of,), jnp.float32, least / len(cuts), top_value / len(cuts))
        return jnp.repeat(jnp.exp(heights), dims[axis_at] // shards_of).reshape((-1,) + (1,) * (len(dims) - axis_at - 1))

    level = one(*cuts[0])
    for cut in cuts[1:]:
        level = level * one(*cut)
    return level


def rank_table(number_of, slope):
    portions = [(1 << 20) // math.isqrt(rank ** slope) + 1 for rank in range(1, number_of + 1)]
    width = 1 + sum(portions) // (1 << 30)
    return np.cumsum(np.array([max(1, weight // width) for weight in portions]))


def ranked(stream_key, shape, amount, skew):
    table = rank_table(amount, skew)
    ticket = jax.random.randint(jax.random.fold_in(stream_key, 1), shape, 0, int(table[amount - 1]))
    standing = jnp.searchsorted(jnp.asarray(table, jnp.int32), ticket, side="right")
    return jax.random.permutation(jax.random.fold_in(stream_key, 2), amount)[standing].astype(jnp.int32)


def shared_out(rng, own, number, rows, number_of, top, bound, skew):
    order = jax.random.permutation(rng, number_of)
    packed, ordinary = load_shares(number_of, rows * top, bound, skew, True), load_shares(number_of, rows * top, bound, skew, False)
    places = jnp.arange(number_of)

    def named(sizes, turn):
        used = int((sizes > 0).sum())
        fixed = max(1, used // 4)
        shifted = fixed + (places - fixed + turn * (used - fixed)) % max(1, number_of - fixed)
        return jnp.zeros((number_of,), jnp.int32).at[order[jnp.where(places < fixed, places, shifted)]].set(jnp.asarray(sizes, jnp.int32))

    sizes = jnp.where(number % 4 == 0, named(packed, number // 4), named(ordinary, number - number // 4 - 1))
    mixed = jax.random.permutation(jax.random.fold_in(own, 3), number_of)
    giver, taker = mixed[0:number_of // 2 * 2:2], mixed[1:number_of // 2 * 2:2]
    room = jnp.minimum(sizes[giver] - 1, bound - sizes[taker]) // 2
    room = jnp.where((giver == order[0]) | (taker == order[0]) | (sizes[taker] == 0), 0, jnp.maximum(room, 0))
    shifted = jax.random.randint(jax.random.fold_in(own, 4), (number_of // 2,), 0, 1 << 20) % (room + 1)
    sizes = sizes.at[giver].add(-shifted).at[taker].add(shifted)
    labels = jnp.searchsorted(jnp.cumsum(sizes), jnp.arange(rows * top), side="right").astype(jnp.int32)
    listing = labels.reshape(top, rows).T
    listing = listing[jax.random.permutation(jax.random.fold_in(own, 1), rows)]
    turn = jax.random.randint(jax.random.fold_in(own, 2), (rows, 1), 0, top)
    return jnp.take_along_axis(listing, (jnp.arange(top)[None, :] + turn) % top, axis=1)


def load_shares(amount, total, limit, lean, full):
    weights = [(1 << 20) // math.isqrt(standing ** lean) + 1 for standing in range(1, amount + 1)]
    largest = limit if full else min(limit, max(-(-total // amount), total * weights[0] // sum(weights)))
    least = 1 if total - largest >= amount - 1 else 0
    counts, surplus = [largest] + [least] * (amount - 1), total - largest - least * (amount - 1)
    while surplus > 0:
        free = [i for i in range(1, amount) if counts[i] < largest] or [i for i in range(1, amount) if counts[i] < limit]
        pool, remaining = sum([weights[i] for i in free]), surplus
        for i in free:
            addition = min(limit - counts[i], max(1, remaining * weights[i] // pool), surplus)
            counts[i] = counts[i] + addition
            surplus = surplus - addition
    return np.array(counts)


def normal_values(own_key, shape, spread, most, shards=(), held_as=jnp.bfloat16):
    entries = spread * jax.random.normal(own_key, shape, jnp.float32)
    if shards:
        entries = entries * block_scale(own_key, shape, shards, -0.22, 0.18)
    return jnp.clip(entries, -most, most).astype(held_as)


def setup_inputs(seed: int = 0) -> dict:
    arg_keys = jax.random.split(jax.random.key(seed), 8)
    table = normal_values(arg_keys[0], (ROWS, E), 1.0, 6.0, ((0, 128),), jnp.float32)
    feature_owner_keys = jax.random.split(jax.random.fold_in(arg_keys[1], 1), PAIRS // PAIRS_DEV)
    feature_owner_turns = jax.random.permutation(jax.random.fold_in(arg_keys[1], 3), PAIRS // PAIRS_DEV)
    feature_owner = jax.vmap(lambda own, number: shared_out(jax.random.fold_in(arg_keys[1], 2), own, number, PAIRS_DEV, N_TABLE * N_DP, 2 * BAG, CAP, 2))(feature_owner_keys, feature_owner_turns).reshape((PAIRS, 2 * BAG))
    feature_offset = set_ends(ranked(arg_keys[2], (PAIRS, 2 * BAG), ROWS_DEV, 2), jax.random.fold_in(arg_keys[2], 3), 0, ROWS_DEV - 1).astype(jnp.int32)
    query_in = normal_values(arg_keys[3], (E, H), E ** -0.5, 0.375)
    query_out = normal_values(arg_keys[4], (H, E), H ** -0.5, 0.1875)
    item_in = normal_values(arg_keys[5], (E, H), E ** -0.5, 0.375)
    item_out = normal_values(arg_keys[6], (H, E), H ** -0.5, 0.1875)
    return {"table": table, "feature_owner": feature_owner, "feature_offset": feature_offset, "query_in": query_in, "query_out": query_out, "item_in": item_in, "item_out": item_out}


score_scale = 20.0

def tower(inputs, w_in, w_out):
    pre_act = jnp.dot(inputs, w_in, preferred_element_type=jnp.float32)
    hidden = jax.nn.silu(pre_act).astype(jnp.bfloat16)
    output = jnp.dot(hidden, w_out, preferred_element_type=jnp.float32)
    out_norm = jnp.sqrt(lax.optimization_barrier(jnp.sum(output * output, axis=-1, keepdims=True)) + 1e-06)
    return (pre_act, hidden, out_norm, output / out_norm)

def tower_back(inputs, w_in, w_out, saved, grad_unit):
    pre_act, hidden, out_norm, unit = saved
    grad_output = ((grad_unit - unit * lax.optimization_barrier(jnp.sum(grad_unit * unit, axis=-1, keepdims=True))) / out_norm).astype(jnp.bfloat16)
    grad_w_out = jnp.dot(hidden.T, grad_output, preferred_element_type=jnp.float32)
    grad_hidden = jnp.dot(grad_output, w_out.T, preferred_element_type=jnp.float32)
    sigmoid_a = jax.nn.sigmoid(pre_act)
    grad_pre = (grad_hidden * sigmoid_a * (1.0 + pre_act * (1.0 - sigmoid_a))).astype(jnp.bfloat16)
    grad_w_in = jnp.dot(inputs.T, grad_pre, preferred_element_type=jnp.float32)
    grad_inputs = jnp.dot(grad_pre, w_in.T, preferred_element_type=jnp.float32)
    return (grad_w_in, grad_w_out, grad_inputs)

def group_scores(queries, items):
    block_rows = math.gcd(BATCH, 1024)
    block_count = BATCH // block_rows
    query_blocks = queries.reshape(block_count, block_rows, E)

    def step(carry, inputs_b):
        index, q_block = inputs_b
        scores = score_scale * jnp.dot(q_block, items.T, preferred_element_type=jnp.float32)
        log_total = jnp.log(lax.optimization_barrier(jnp.sum(jnp.exp(scores), axis=1)))
        start_col = (index * block_rows).astype(jnp.int32)
        own_part = lax.dynamic_slice_in_dim(scores, start_col, block_rows, 1)
        loss_block = log_total - jnp.diagonal(own_part)
        soft = jnp.exp(scores - log_total[:, None]).astype(jnp.bfloat16)
        k_block = lax.dynamic_slice_in_dim(items, start_col, block_rows, 0)
        grad_q = score_scale * (jnp.dot(soft, items, preferred_element_type=jnp.float32) - k_block.astype(jnp.float32))
        carry = carry + jnp.dot(soft.T, q_block, preferred_element_type=jnp.float32)
        return (carry, (loss_block, grad_q))
    start_acc = jnp.zeros((BATCH, E), jnp.float32)
    acc_total, (loss_all, grad_q_all) = lax.scan(step, start_acc, (jnp.arange(block_count, dtype=jnp.int32), query_blocks))
    grad_k = score_scale * (acc_total - queries.astype(jnp.float32))
    return (loss_all.reshape(BATCH), grad_q_all.reshape(BATCH, E), grad_k)

def reference(table, feature_owner, feature_offset, query_in, query_out, item_in, item_out):
    ids = feature_owner * ROWS_DEV + feature_offset
    looked_up = table[ids].astype(jnp.bfloat16)
    query_x = lax.optimization_barrier(jnp.sum(looked_up[:, :BAG].astype(jnp.float32), axis=1)).astype(jnp.bfloat16)
    item_x = lax.optimization_barrier(jnp.sum(looked_up[:, BAG:].astype(jnp.float32), axis=1)).astype(jnp.bfloat16)
    q_saved = tower(query_x, query_in, query_out)
    k_saved = tower(item_x, item_in, item_out)
    query_unit = q_saved[3].astype(jnp.bfloat16)
    item_unit = k_saved[3].astype(jnp.bfloat16)
    loss_g, grad_q_g, grad_k_g = lax.map(lambda pair_in: group_scores(pair_in[0], pair_in[1]), (query_unit.reshape(N_TABLE, BATCH, E), item_unit.reshape(N_TABLE, BATCH, E)))
    loss = loss_g.reshape(PAIRS)
    grad_query = grad_q_g.reshape(PAIRS, E)
    grad_item = grad_k_g.reshape(PAIRS, E)
    q_win, q_wout, q_dx = tower_back(query_x, query_in, query_out, q_saved, grad_query)
    k_win, k_wout, k_dx = tower_back(item_x, item_in, item_out, k_saved, grad_item)
    row_grads = jnp.concatenate([jnp.broadcast_to(q_dx[:, None, :], (PAIRS, BAG, E)), jnp.broadcast_to(k_dx[:, None, :], (PAIRS, BAG, E))], axis=1)
    table_grad = jnp.zeros((ROWS, E), jnp.float32).at[ids.reshape(-1)].add(row_grads.reshape(-1, E))
    return (loss, table_grad, q_win, q_wout, k_win, k_wout)
```

```python
import functools

import jax
import jax.numpy as jnp
from jax import lax
from jax.experimental import pallas as pl
from jax.experimental.pallas import tpu as pltpu
from jax.sharding import PartitionSpec as P

score_scale = 20.0
MESH = pl.DeviceIdType.MESH
CAP = 16


def fetch_kernel(
    shards, group, requests, table_ref, fetched, asked,
    table_rows, rows, stage, asked_scalars, table_sem, id_sems, scalar_sem, row_sems,
):
    me = lax.axis_index("table") * group + lax.axis_index("dp")
    load = pltpu.make_async_copy(table_ref, table_rows, table_sem)
    load.start()

    def place(device):
        return (lax.div(device, group), lax.rem(device, group))

    barrier = pltpu.get_barrier_semaphore()

    @pl.loop(1, shards)
    def _(step):
        pl.semaphore_signal(
            barrier, inc=1, device_id=place(lax.rem(me + step, shards)), device_id_type=MESH
        )

    pl.semaphore_wait(barrier, shards - 1)
    pltpu.make_async_copy(requests.at[me], asked.at[me], scalar_sem).start()

    @pl.loop(1, shards)
    def _(step):
        owner = lax.rem(me + step, shards)
        pltpu.make_async_remote_copy(
            requests.at[owner], asked.at[me], id_sems.at[0], id_sems.at[1],
            device_id=place(owner), device_id_type=MESH,
        ).start()

    others = pl.ds(0, shards - 1)
    pltpu.make_async_copy(requests.at[me], asked.at[me], scalar_sem).wait()
    pltpu.make_async_copy(asked.at[others], asked.at[others], id_sems.at[1]).wait()
    spread = pltpu.make_async_copy(asked, asked_scalars, scalar_sem)
    spread.start()
    load.wait()
    spread.wait()

    def lookup(asker):
        for slot in range(CAP):
            stage[slot : slot + 1, :] = table_rows[pl.ds(asked_scalars[asker, 0, slot], 1), :]
        return stage[...].astype(jnp.bfloat16)

    @pl.loop(1, shards)
    def _(step):
        asker = lax.rem(me + step, shards)
        rows[asker] = lookup(asker)
        pltpu.make_async_remote_copy(
            rows.at[asker], fetched.at[me], row_sems.at[0], row_sems.at[1],
            device_id=place(asker), device_id_type=MESH,
        ).start()

    fetched[me] = lookup(me)
    pltpu.make_async_copy(requests.at[others], requests.at[others], id_sems.at[0]).wait()
    pltpu.make_async_copy(rows.at[others], rows.at[others], row_sems.at[1]).wait()
    pltpu.make_async_copy(rows.at[others], rows.at[others], row_sems.at[0]).wait()


def fetch(requests, table):
    group = lax.axis_size("dp")
    shards = lax.axis_size("table") * group
    width = table.shape[1]
    return pl.pallas_call(
        functools.partial(fetch_kernel, shards, group),
        out_shape=(
            jax.ShapeDtypeStruct((shards, CAP, width), jnp.bfloat16),
            jax.ShapeDtypeStruct((shards, 1, 128), jnp.int32),
        ),
        in_specs=[pl.BlockSpec(memory_space=pltpu.VMEM), pl.BlockSpec(memory_space=pl.ANY)],
        out_specs=(pl.BlockSpec(memory_space=pltpu.VMEM),) * 2,
        scratch_shapes=[
            pltpu.VMEM(table.shape, jnp.float32),
            pltpu.VMEM((shards, CAP, width), jnp.bfloat16),
            pltpu.VMEM((CAP, width), jnp.float32),
            pltpu.SMEM((shards, 1, 128), jnp.int32),
            pltpu.SemaphoreType.DMA,
            pltpu.SemaphoreType.DMA((2,)),
            pltpu.SemaphoreType.DMA,
            pltpu.SemaphoreType.DMA((2,)),
        ],
        compiler_params=pltpu.CompilerParams(
            collective_id=0, has_side_effects=True, vmem_limit_bytes=24 << 20
        ),
    )(requests, table)


def tower(inputs, w_in, w_out):
    pre_act = jnp.dot(inputs, w_in, preferred_element_type=jnp.float32)
    hidden = jax.nn.silu(pre_act).astype(jnp.bfloat16)
    output = jnp.dot(hidden, w_out, preferred_element_type=jnp.float32)
    out_norm = jnp.sqrt(jnp.sum(output * output, axis=-1, keepdims=True) + 1e-06)
    return (pre_act, hidden, out_norm, output / out_norm)


def tower_back(inputs, w_in, w_out, saved, grad_unit):
    pre_act, hidden, out_norm, unit = saved
    grad_output = (
        (grad_unit - unit * jnp.sum(grad_unit * unit, axis=-1, keepdims=True)) / out_norm
    ).astype(jnp.bfloat16)
    grad_w_out = jnp.dot(hidden.T, grad_output, preferred_element_type=jnp.float32)
    grad_hidden = jnp.dot(grad_output, w_out.T, preferred_element_type=jnp.float32)
    sigmoid_a = jax.nn.sigmoid(pre_act)
    grad_pre = (grad_hidden * sigmoid_a * (1.0 + pre_act * (1.0 - sigmoid_a))).astype(jnp.bfloat16)
    grad_w_in = jnp.dot(inputs.T, grad_pre, preferred_element_type=jnp.float32)
    grad_inputs = jnp.dot(grad_pre, w_in.T, preferred_element_type=jnp.float32)
    return (grad_w_in, grad_w_out, grad_inputs)


def local(table, feature_owner, feature_offset, query_in, query_out, item_in, item_out):
    pair_count = feature_owner.shape[0]
    per_pair = feature_owner.shape[1]
    bag_size = per_pair // 2
    feat_width = table.shape[1]
    table_devs = lax.axis_size("table")
    group_devs = lax.axis_size("dp")
    shards = table_devs * group_devs
    id_count = pair_count * per_pair
    slot_cap = 2 * id_count // shards
    flat_owner = feature_owner.reshape(-1)
    flat_offset = feature_offset.reshape(-1)
    one_hot = (flat_owner[:, None] == jnp.arange(shards, dtype=jnp.int32)[None, :]).astype(
        jnp.int32
    )
    slot_rank = jnp.sum((jnp.cumsum(one_hot, axis=0) - 1) * one_hot, axis=1)
    position = flat_owner * slot_cap + slot_rank
    requests = (
        jnp.zeros((shards * slot_cap,), jnp.int32)
        .at[position]
        .set(flat_offset)
        .reshape(shards, slot_cap)
    )
    fetched, asked = fetch(
        jnp.pad(requests, ((0, 0), (0, 128 - slot_cap))).reshape(shards, 1, 128), table
    )
    asked_piece = asked[:, 0, :slot_cap]
    pair_rows = fetched.reshape(shards * slot_cap, feat_width)[position].reshape(
        pair_count, per_pair, feat_width
    )
    query_x = jnp.sum(pair_rows[:, :bag_size].astype(jnp.float32), axis=1).astype(jnp.bfloat16)
    item_x = jnp.sum(pair_rows[:, bag_size:].astype(jnp.float32), axis=1).astype(jnp.bfloat16)
    q_saved = tower(query_x, query_in, query_out)
    k_saved = tower(item_x, item_in, item_out)
    query_unit = q_saved[3].astype(jnp.bfloat16)
    item_unit = k_saved[3].astype(jnp.bfloat16)
    all_items = lax.all_gather(item_unit, "dp", axis=0, tiled=True)
    scores = score_scale * jnp.dot(query_unit, all_items.T, preferred_element_type=jnp.float32)
    log_total = jnp.log(jnp.sum(jnp.exp(scores), axis=1))
    own_start = lax.axis_index("dp") * pair_count
    own_part = lax.dynamic_slice_in_dim(scores, own_start, pair_count, 1)
    loss = log_total - jnp.diagonal(own_part)
    soft = jnp.exp(scores - log_total[:, None]).astype(jnp.bfloat16)
    grad_query = score_scale * (
        jnp.dot(soft, all_items, preferred_element_type=jnp.float32) - item_unit.astype(jnp.float32)
    )
    summed = lax.psum_scatter(
        jnp.dot(soft.T, query_unit, preferred_element_type=jnp.float32).astype(jnp.bfloat16),
        "dp",
        scatter_dimension=0,
        tiled=True,
    ).astype(jnp.float32)
    grad_item = score_scale * (summed - query_unit.astype(jnp.float32))
    q_win, q_wout, q_dx = tower_back(query_x, query_in, query_out, q_saved, grad_query)
    k_win, k_wout, k_dx = tower_back(item_x, item_in, item_out, k_saved, grad_item)
    q_win, q_wout, k_win, k_wout = lax.psum((q_win, q_wout, k_win, k_wout), ("table", "dp"))
    row_grads = jnp.concatenate(
        [
            jnp.broadcast_to(q_dx[:, None, :], (pair_count, bag_size, feat_width)),
            jnp.broadcast_to(k_dx[:, None, :], (pair_count, bag_size, feat_width)),
        ],
        axis=1,
    )
    grad_slots = (
        jnp.zeros((shards * slot_cap, feat_width), jnp.float32)
        .at[position]
        .set(row_grads.reshape(-1, feat_width))
    )
    returned = lax.all_to_all(
        grad_slots.reshape(shards, slot_cap, feat_width).astype(jnp.bfloat16),
        ("table", "dp"),
        split_axis=0,
        concat_axis=0,
        tiled=True,
    ).astype(jnp.float32)
    table_grad = (
        jnp.zeros(table.shape, jnp.float32)
        .at[asked_piece.reshape(-1)]
        .add(returned.reshape(-1, feat_width))
    )
    return (loss, table_grad, q_win, q_wout, k_win, k_wout)


def solution(mesh):
    in_specs = (
        P(("table", "dp"), None),
        P(("table", "dp"), None),
        P(("table", "dp"), None),
        P(),
        P(),
        P(),
        P(),
    )
    out_specs = (P(("table", "dp")), P(("table", "dp"), None), P(), P(), P(), P())
    return jax.shard_map(local, mesh=mesh, in_specs=in_specs, out_specs=out_specs, check_vma=False)
```

```python
import jax
import jax.numpy as jnp
from jax import lax
from jax.experimental import pallas as pl
from jax.experimental.pallas import tpu as pltpu
from jax.sharding import PartitionSpec as P

MESH = pl.DeviceIdType.MESH
SCALE = 20.0
SHARDS = 128
GROUP = 32
CAP = 16
PAIRS = 128
WIDTH = 256
HIDDEN = 1024
ROWS = 8192
QUERY_PEERS = 8
ITEM_PEERS = 4
BLOCK_Q = QUERY_PEERS * PAIRS
BLOCK_K = ITEM_PEERS * PAIRS
GRAD_ROWS = 4 * HIDDEN
HALF = GRAD_ROWS // 2
PARTS = ((0, 768, (0, 1, 2)), (768, 768, (2, 0, 1)), (1536, 512, (1, 2, 0)))
f32 = jnp.float32
bf16 = jnp.bfloat16


def mm(a, b, contract=((1,), (0,))):
    return lax.dot_general(a, b, (contract, ((), ())), preferred_element_type=f32)


def step_kernel(
    owner_ref, offset_ref, table_ref, w_ins_ref, w_outs_ref, w_ini_ref, w_outi_ref,
    loss_ref, asked, returned, summed,
    table_rows, w_in, w_out, requests, asked_scalars, stage, rows, fetched, pick, pick_t,
    pre_act, hidden, unit, norm, queries, items, expo, soft, part_sums,
    q_send, q_recv, k_send, k_recv, slots, grads, core_recv, half, sum1, recv1, recv2, recv3,
    load_sems, send_sems, recv_sems, ring_send, ring_recv,
):
    t = lax.axis_index("table")
    dp = lax.axis_index("dp")
    me = t * GROUP + dp
    core = lax.rem(t, 2)
    z = lax.div(dp, QUERY_PEERS)
    a = lax.rem(dp, QUERY_PEERS)
    x = lax.div(a, 2)
    y = lax.rem(a, 2) * 2 + lax.div(t, 2)
    coords = (x, y, z)

    def place(device):
        return (lax.div(device, GROUP), lax.rem(device, GROUP))

    def chip(coords, core):
        cx, cy, cz = coords
        return (lax.rem(cy, 2) * 2 + core, cz * QUERY_PEERS + cx * 2 + lax.div(cy, 2))

    def send(src, dst, s_sem, r_sem, device):
        pltpu.make_async_remote_copy(
            src, dst, s_sem, r_sem, device_id=device, device_id_type=MESH
        ).start()

    def wait(ref, sem):
        pltpu.make_async_copy(ref, ref, sem).wait()

    loads = [
        pltpu.make_async_copy(src, dst, load_sems.at[i])
        for i, (src, dst) in enumerate(
            [
                (table_ref, table_rows),
                (w_ins_ref, w_in.at[0]),
                (w_outs_ref, w_out.at[0]),
                (w_ini_ref, w_in.at[1]),
                (w_outi_ref, w_out.at[1]),
            ]
        )
    ]
    for load in loads:
        load.start()

    barrier = pltpu.get_barrier_semaphore()

    @pl.loop(1, SHARDS)
    def _(step):
        pl.semaphore_signal(
            barrier, inc=1, device_id=place(lax.rem(me + step, SHARDS)), device_id_type=MESH
        )

    lane = lax.broadcasted_iota(jnp.int32, (PAIRS, SHARDS), 1)
    row = lax.broadcasted_iota(jnp.int32, (PAIRS, SHARDS), 0)
    names = [(owner_ref[:, k : k + 1] == lane).astype(jnp.int32) for k in range(8)]
    offsets = sum(names[k] * offset_ref[:, k : k + 1] for k in range(8))
    named_q = sum(names[:4])
    named_k = sum(names[4:])
    named = named_q + named_k
    rank = named
    for shift in (1, 2, 4, 8, 16, 32, 64):
        rank = rank + jnp.where(row >= shift, pltpu.roll(rank, shift, 0), 0)
    rank = rank - named
    by_slot = [
        jnp.sum(jnp.where(rank == r, offsets, 0), axis=0, keepdims=True) for r in range(CAP)
    ] + [jnp.sum(named, axis=0, keepdims=True)]
    by_slot = jnp.concatenate(
        by_slot + [jnp.zeros((SHARDS - CAP - 1, SHARDS), jnp.int32)], axis=0
    )
    requests[...] = by_slot.T.reshape(SHARDS, 1, SHARDS)

    pl.semaphore_wait(barrier, SHARDS - 1)

    others = pl.ds(0, SHARDS - 1)
    asked[me] = requests[me]

    @pl.loop(1, SHARDS)
    def _(step):
        d = lax.rem(me + step, SHARDS)
        send(requests.at[d], asked.at[me], send_sems.at[0], recv_sems.at[0], place(d))

    wait(asked.at[others], recv_sems.at[0])
    spread = pltpu.make_async_copy(asked, asked_scalars, load_sems.at[5])
    spread.start()
    loads[0].wait()
    spread.wait()

    def lookup(d):
        for slot in range(CAP):
            stage[slot : slot + 1, :] = table_rows[pl.ds(asked_scalars[d, 0, slot], 1), :]
        return stage[...].astype(bf16)

    @pl.loop(1, SHARDS)
    def _(step):
        d = lax.rem(me + step, SHARDS)
        rows[d] = lookup(d)
        send(rows.at[d], fetched.at[me], send_sems.at[1], recv_sems.at[1], place(d))

    fetched[me] = lookup(me)

    cut = 512
    rank_b, named_qb, named_kb = (v.astype(f32).astype(bf16) for v in (rank, named_q, named_k))
    for c in range(SHARDS * CAP // cut):
        col = lax.broadcasted_iota(jnp.int32, (SHARDS, cut), 1) + c * cut
        dev = lax.broadcasted_iota(jnp.int32, (SHARDS, cut), 0)
        spread_b = (lax.div(col, CAP) == dev).astype(bf16)
        hit = mm(rank_b, spread_b) == lax.rem(col, CAP).astype(f32)
        pick[0:PAIRS, c * cut : (c + 1) * cut] = jnp.where(hit, mm(named_qb, spread_b), 0.0).astype(bf16)
        pick[PAIRS:, c * cut : (c + 1) * cut] = jnp.where(hit, mm(named_kb, spread_b), 0.0).astype(bf16)
        col = lax.broadcasted_iota(jnp.int32, (cut, SHARDS), 0) + c * cut
        dev = lax.broadcasted_iota(jnp.int32, (cut, SHARDS), 1)
        spread_b = (lax.div(col, CAP) == dev).astype(bf16)
        rhs_t = ((1,), (1,))
        hit = mm(spread_b, rank_b, rhs_t) == lax.rem(col, CAP).astype(f32)
        pick_t[c * cut : (c + 1) * cut, 0:PAIRS] = jnp.where(hit, mm(spread_b, named_qb, rhs_t), 0.0).astype(bf16)
        pick_t[c * cut : (c + 1) * cut, PAIRS:] = jnp.where(hit, mm(spread_b, named_kb, rhs_t), 0.0).astype(bf16)

    for load in loads[1:]:
        load.wait()
    wait(rows.at[others], recv_sems.at[1])
    inputs = mm(pick[...], fetched[...].reshape(SHARDS * CAP, WIDTH)).astype(bf16)
    x_in = (inputs[0:PAIRS], inputs[PAIRS:])

    for i in range(2):
        pre = mm(x_in[i], w_in[i])
        pre_act[i] = pre
        hid = (pre * lax.logistic(pre)).astype(bf16)
        hidden[i] = hid
        out = mm(hid, w_out[i])
        out_norm = jnp.sqrt(jnp.sum(out * out, axis=-1, keepdims=True) + 1e-06)
        unit[i] = out / out_norm
        norm[i] = jnp.broadcast_to(out_norm, (PAIRS, WIDTH))
        if i == 0:
            queries[a] = unit[0].astype(bf16)
            for j in range(1, QUERY_PEERS):
                peer = (t, z * QUERY_PEERS + lax.rem(a + j, QUERY_PEERS))
                send(queries.at[a], queries.at[a], send_sems.at[2], recv_sems.at[2], peer)
        else:
            items[z] = unit[1].astype(bf16)
            for j in range(1, ITEM_PEERS):
                peer = (t, lax.rem(z + j, ITEM_PEERS) * QUERY_PEERS + a)
                send(items.at[z], items.at[z], send_sems.at[3], recv_sems.at[3], peer)
    query_unit = queries[a].astype(f32)
    item_unit = items[z].astype(f32)
    wait(items.at[pl.ds(0, ITEM_PEERS - 1)], recv_sems.at[3])
    wait(queries.at[pl.ds(0, QUERY_PEERS - 1)], recv_sems.at[2])

    all_items = items[...].reshape(BLOCK_K, WIDTH)
    sums = []
    for c in range(QUERY_PEERS):
        e = jnp.exp(SCALE * mm(all_items, queries[c], ((1,), (1,))))
        expo[:, c * PAIRS : (c + 1) * PAIRS] = e
        sums.append(jnp.sum(e, axis=0, keepdims=True))
    part_sums[a] = jnp.concatenate(sums, axis=0)
    for j in range(1, QUERY_PEERS):
        peer = (t, z * QUERY_PEERS + lax.rem(a + j, QUERY_PEERS))
        send(part_sums.at[a], part_sums.at[a], send_sems.at[4], recv_sems.at[4], peer)
    own_score = SCALE * jnp.sum(query_unit * item_unit, axis=1, keepdims=True)
    own_score = jnp.sum(jnp.where(lane == row, own_score, 0.0), axis=0, keepdims=True)
    wait(part_sums.at[pl.ds(0, QUERY_PEERS - 1)], recv_sems.at[4])
    total = part_sums[0]
    for c in range(1, QUERY_PEERS):
        total = total + part_sums[c]
    mine = lax.broadcasted_iota(jnp.int32, (QUERY_PEERS, PAIRS), 0) == a
    own_total = jnp.sum(jnp.where(mine, total, 0.0), axis=0, keepdims=True)
    loss_ref[...] = jnp.log(own_total) - own_score
    inverse = 1.0 / total
    for c in range(QUERY_PEERS):
        at = slice(c * PAIRS, (c + 1) * PAIRS)
        soft[:, at] = (expo[:, at] * inverse[c : c + 1, :]).astype(bf16)

    def part_q(c):
        block = soft[:, pl.ds(pl.multiple_of(c * PAIRS, PAIRS), PAIRS)]
        return mm(block, all_items, ((0,), (0,)))

    def part_k(c):
        block = soft[pl.ds(pl.multiple_of(c * PAIRS, PAIRS), PAIRS), :]
        return mm(block, queries[...].reshape(BLOCK_Q, WIDTH))

    for j in range(1, QUERY_PEERS):
        c = lax.rem(a + j, QUERY_PEERS)
        q_send[j - 1] = part_q(c).astype(bf16)
        send(q_send.at[j - 1], q_recv.at[j - 1], send_sems.at[5], recv_sems.at[5], (t, z * QUERY_PEERS + c))
    for j in range(1, ITEM_PEERS):
        c = lax.rem(z + j, ITEM_PEERS)
        k_send[j - 1] = part_k(c).astype(bf16)
        send(k_send.at[j - 1], k_recv.at[j - 1], send_sems.at[6], recv_sems.at[6], (t, c * QUERY_PEERS + a))
    grad_q = part_q(a) - item_unit
    grad_k = part_k(z) - query_unit
    wait(q_recv, recv_sems.at[5])
    for j in range(QUERY_PEERS - 1):
        grad_q = grad_q + q_recv[j].astype(f32)
    wait(k_recv, recv_sems.at[6])
    for j in range(ITEM_PEERS - 1):
        grad_k = grad_k + k_recv[j].astype(f32)

    grad_out, grad_pre, grad_x = [], [], []
    for i, grad_unit in enumerate((SCALE * grad_q, SCALE * grad_k)):
        u = unit[i]
        g = ((grad_unit - u * jnp.sum(grad_unit * u, axis=-1, keepdims=True)) / norm[i]).astype(bf16)
        grad_hidden = mm(g, w_out[i], ((1,), (1,)))
        pre = pre_act[i]
        s = lax.logistic(pre)
        gp = (grad_hidden * s * (1.0 + pre * (1.0 - s))).astype(bf16)
        grad_out.append(g)
        grad_pre.append(gp)
        grad_x.append(mm(gp, w_in[i], ((1,), (1,))).astype(bf16))

    slots[...] = (
        mm(pick_t[...], jnp.concatenate(grad_x, axis=0)).astype(bf16).reshape(SHARDS, CAP, WIDTH)
    )

    @pl.loop(1, SHARDS)
    def _(step):
        d = lax.rem(me + step, SHARDS)
        send(slots.at[d], returned.at[me], send_sems.at[7], recv_sems.at[7], place(d))

    returned[me] = slots[me]

    for i in range(2):
        base = i * HALF
        for c in range(0, HIDDEN, WIDTH):
            grads[base + c : base + c + WIDTH] = mm(
                x_in[i], grad_pre[i][:, c : c + WIDTH], ((0,), (0,))
            ).astype(bf16)
        base += HIDDEN
        for c in range(0, HIDDEN, WIDTH):
            grads[base + c : base + c + WIDTH] = mm(
                hidden[i, :, c : c + WIDTH], grad_out[i], ((0,), (0,))
            ).astype(bf16)

    def half_at(c):
        return pl.ds(pl.multiple_of(c * HALF, HALF), HALF)

    send(grads.at[half_at(1 - core)], core_recv, send_sems.at[8], recv_sems.at[8], chip(coords, 1 - core))
    wait(core_recv, recv_sems.at[8])
    half[...] = (grads[half_at(core)].astype(f32) + core_recv[...].astype(f32)).astype(bf16)

    def along(axis, j):
        moved = list(coords)
        moved[axis] = lax.rem(coords[axis] + j, 4)
        return moved[axis], chip(moved, core)

    def rows_at(start, size):
        return pl.ds(pl.multiple_of(start, 16), size)

    at1, at2 = 0, 0
    spans = []
    for base, size, _ in PARTS:
        spans.append((at1, at2))
        at1, at2 = at1 + size // 4, at2 + size // 16
    for p, (base, size, axes) in enumerate(PARTS):
        n = size // 4
        for j in range(1, 4):
            c, device = along(axes[0], j)
            send(half.at[rows_at(base + c * n, n)], recv1.at[j - 1, pl.ds(spans[p][0], n)],
                 ring_send.at[p, 0], ring_recv.at[p, 0], device)
    for p, (base, size, axes) in enumerate(PARTS):
        n, m = size // 4, size // 16
        at = pl.ds(spans[p][0], n)
        wait(recv1.at[:, at], ring_recv.at[p, 0])
        total1 = half[rows_at(base + coords[axes[0]] * n, n)].astype(f32)
        for j in range(3):
            total1 = total1 + recv1[j, at].astype(f32)
        sum1[at] = total1.astype(bf16)
        for j in range(1, 4):
            c, device = along(axes[1], j)
            send(sum1.at[rows_at(spans[p][0] + c * m, m)], recv2.at[j - 1, pl.ds(spans[p][1], m)],
                 ring_send.at[p, 1], ring_recv.at[p, 1], device)
    for p, (base, size, axes) in enumerate(PARTS):
        m = size // 16
        at = pl.ds(spans[p][1], m)
        wait(recv2.at[:, at], ring_recv.at[p, 1])
        total2 = sum1[rows_at(spans[p][0] + coords[axes[1]] * m, m)].astype(f32)
        for j in range(3):
            total2 = total2 + recv2[j, at].astype(f32)
        c3 = coords[axes[2]]
        recv3[c3, at] = total2.astype(bf16)
        for j in range(1, 4):
            _, device = along(axes[2], j)
            send(recv3.at[c3, at], recv3.at[c3, at], ring_send.at[p, 2], ring_recv.at[p, 2], device)
    for p, (base, size, axes) in enumerate(PARTS):
        n, m = size // 4, size // 16
        at = pl.ds(spans[p][1], m)
        wait(recv3.at[pl.ds(0, 3), at], ring_recv.at[p, 2])
        total3 = recv3[0, at].astype(f32)
        for j in range(1, 4):
            total3 = total3 + recv3[j, at].astype(f32)
        mine = rows_at(core * HALF + base + coords[axes[0]] * n + coords[axes[1]] * m, m)
        summed[mine] = total3.astype(bf16)
        for j in range(1, 4):
            _, device = along(axes[1], j)
            send(summed.at[mine], summed.at[mine], ring_send.at[p, 3], ring_recv.at[p, 3], device)
    for p, (base, size, axes) in enumerate(PARTS):
        n, m = size // 4, size // 16
        wait(summed.at[pl.ds(0, 3 * m)], ring_recv.at[p, 3])
        mine = rows_at(core * HALF + base + coords[axes[0]] * n, n)
        for j in range(1, 4):
            _, device = along(axes[0], j)
            send(summed.at[mine], summed.at[mine], ring_send.at[p, 4], ring_recv.at[p, 4], device)
    for p, (base, size, axes) in enumerate(PARTS):
        n = size // 4
        wait(summed.at[pl.ds(0, 3 * n)], ring_recv.at[p, 4])
        mine = rows_at(core * HALF + base, size)
        send(summed.at[mine], summed.at[mine], ring_send.at[p, 5], ring_recv.at[p, 5], chip(coords, 1 - core))
    for p, (base, size, axes) in enumerate(PARTS):
        wait(summed.at[pl.ds(0, size)], ring_recv.at[p, 5])

    wait(rows.at[others], recv_sems.at[7])
    for ref, i in (
        (requests.at[others], 0),
        (rows.at[others], 1),
        (queries.at[pl.ds(0, QUERY_PEERS - 1)], 2),
        (items.at[pl.ds(0, ITEM_PEERS - 1)], 3),
        (part_sums.at[pl.ds(0, QUERY_PEERS - 1)], 4),
        (q_send, 5),
        (k_send, 6),
        (slots.at[others], 7),
        (core_recv, 8),
    ):
        wait(ref, send_sems.at[i])
    for p, (base, size, axes) in enumerate(PARTS):
        n, m = size // 4, size // 16
        for i, count in enumerate((3 * n, 3 * m, 3 * m, 3 * m, 3 * n, size)):
            wait(summed.at[pl.ds(0, count)], ring_send.at[p, i])


def train_step(owner, offset, table, query_in, query_out, item_in, item_out):
    rows1 = sum(size // 4 for _, size, _ in PARTS)
    rows2 = sum(size // 16 for _, size, _ in PARTS)
    vmem = pl.BlockSpec(memory_space=pltpu.VMEM)
    hbm = pl.BlockSpec(memory_space=pl.ANY)
    V = pltpu.VMEM
    return pl.pallas_call(
        step_kernel,
        out_shape=(
            jax.ShapeDtypeStruct((1, PAIRS), f32),
            jax.ShapeDtypeStruct((SHARDS, 1, SHARDS), jnp.int32),
            jax.ShapeDtypeStruct((SHARDS, CAP, WIDTH), bf16),
            jax.ShapeDtypeStruct((GRAD_ROWS, WIDTH), bf16),
        ),
        in_specs=[vmem, vmem, hbm, hbm, hbm, hbm, hbm],
        out_specs=(vmem,) * 4,
        scratch_shapes=[
            V((ROWS, WIDTH), f32),
            V((2, WIDTH, HIDDEN), bf16),
            V((2, HIDDEN, WIDTH), bf16),
            V((SHARDS, 1, SHARDS), jnp.int32),
            pltpu.SMEM((SHARDS, 1, SHARDS), jnp.int32),
            V((CAP, WIDTH), f32),
            V((SHARDS, CAP, WIDTH), bf16),
            V((SHARDS, CAP, WIDTH), bf16),
            V((2 * PAIRS, SHARDS * CAP), bf16),
            V((SHARDS * CAP, 2 * PAIRS), bf16),
            V((2, PAIRS, HIDDEN), f32),
            V((2, PAIRS, HIDDEN), bf16),
            V((2, PAIRS, WIDTH), f32),
            V((2, PAIRS, WIDTH), f32),
            V((QUERY_PEERS, PAIRS, WIDTH), bf16),
            V((ITEM_PEERS, PAIRS, WIDTH), bf16),
            V((BLOCK_K, BLOCK_Q), f32),
            V((BLOCK_K, BLOCK_Q), bf16),
            V((QUERY_PEERS, QUERY_PEERS, PAIRS), f32),
            V((QUERY_PEERS - 1, PAIRS, WIDTH), bf16),
            V((QUERY_PEERS - 1, PAIRS, WIDTH), bf16),
            V((ITEM_PEERS - 1, PAIRS, WIDTH), bf16),
            V((ITEM_PEERS - 1, PAIRS, WIDTH), bf16),
            V((SHARDS, CAP, WIDTH), bf16),
            V((GRAD_ROWS, WIDTH), bf16),
            V((HALF, WIDTH), bf16),
            V((HALF, WIDTH), bf16),
            V((rows1, WIDTH), bf16),
            V((3, rows1, WIDTH), bf16),
            V((3, rows2, WIDTH), bf16),
            V((4, rows2, WIDTH), bf16),
            pltpu.SemaphoreType.DMA((6,)),
            pltpu.SemaphoreType.DMA((9,)),
            pltpu.SemaphoreType.DMA((9,)),
            pltpu.SemaphoreType.DMA((len(PARTS), 6)),
            pltpu.SemaphoreType.DMA((len(PARTS), 6)),
        ],
        compiler_params=pltpu.CompilerParams(
            collective_id=0, has_side_effects=True, vmem_limit_bytes=56 << 20
        ),
    )(owner, offset, table, query_in, query_out, item_in, item_out)


def update_kernel(
    asked, returned, summed, table_grad, q_in, q_out, k_in, k_out,
    total, wide_in, wide_out, stage, sems,
):
    copies = []
    for i, (out_in, out_out) in enumerate(((q_in, q_out), (k_in, k_out))):
        base = i * HALF
        for c in range(0, HIDDEN, WIDTH):
            wide_in[i, :, c : c + WIDTH] = summed[base + c : base + c + WIDTH].astype(f32)
        wide_out[i] = summed[base + HIDDEN : base + HALF].astype(f32)
        copies.append(pltpu.make_async_copy(wide_in.at[i], out_in, sems.at[2 * i]))
        copies.append(pltpu.make_async_copy(wide_out.at[i], out_out, sems.at[2 * i + 1]))
        copies[-2].start()
        copies[-1].start()

    @pl.loop(0, ROWS, step=256)
    def _(r):
        total[pl.ds(r, 256), :] = jnp.zeros((256, WIDTH), f32)

    @pl.loop(0, SHARDS)
    def _(d):
        stage[...] = returned[d].astype(f32)
        for slot in range(CAP):
            at = pl.ds(asked[d, 0, slot], 1)
            total[at, :] += stage[slot : slot + 1, :]

    last = pltpu.make_async_copy(total, table_grad, sems.at[4])
    last.start()
    for copy in copies:
        copy.wait()
    last.wait()


def update(asked, returned, summed):
    vmem = pl.BlockSpec(memory_space=pltpu.VMEM)
    hbm = pl.BlockSpec(memory_space=pl.ANY)
    in_shape = jax.ShapeDtypeStruct((WIDTH, HIDDEN), f32)
    out_shape = jax.ShapeDtypeStruct((HIDDEN, WIDTH), f32)
    return pl.pallas_call(
        update_kernel,
        out_shape=(jax.ShapeDtypeStruct((ROWS, WIDTH), f32), in_shape, out_shape, in_shape, out_shape),
        in_specs=[pl.BlockSpec(memory_space=pltpu.SMEM), vmem, vmem],
        out_specs=(hbm,) * 5,
        scratch_shapes=[
            pltpu.VMEM((ROWS, WIDTH), f32),
            pltpu.VMEM((2, WIDTH, HIDDEN), f32),
            pltpu.VMEM((2, HIDDEN, WIDTH), f32),
            pltpu.VMEM((CAP, WIDTH), f32),
            pltpu.SemaphoreType.DMA((5,)),
        ],
        compiler_params=pltpu.CompilerParams(vmem_limit_bytes=40 << 20),
    )(asked, returned, summed)


def local(table, feature_owner, feature_offset, query_in, query_out, item_in, item_out):
    loss, asked, returned, summed = train_step(
        feature_owner, feature_offset, table, query_in, query_out, item_in, item_out
    )
    table_grad, q_in, q_out, k_in, k_out = update(asked, returned, summed)
    return (loss.reshape(PAIRS), table_grad, q_in, q_out, k_in, k_out)


def solution(mesh):
    in_specs = (
        P(("table", "dp"), None),
        P(("table", "dp"), None),
        P(("table", "dp"), None),
        P(),
        P(),
        P(),
        P(),
    )
    out_specs = (P(("table", "dp")), P(("table", "dp"), None), P(), P(), P(), P())
    return jax.shard_map(local, mesh=mesh, in_specs=in_specs, out_specs=out_specs, check_vma=False)
```

```python
import jax
import jax.numpy as jnp
from jax import lax
from jax.experimental import pallas as pl
from jax.experimental.pallas import tpu as pltpu
from jax.sharding import PartitionSpec as P

MESH = pl.DeviceIdType.MESH
SCALE = 20.0
SHARDS = 128
GROUP = 32
CAP = 16
PAIRS = 128
WIDTH = 256
HIDDEN = 1024
ROWS = 8192
QUERY_PEERS = 8
ITEM_PEERS = 4
BLOCK_Q = QUERY_PEERS * PAIRS
BLOCK_K = ITEM_PEERS * PAIRS
GRAD_ROWS = 4 * HIDDEN
HALF = GRAD_ROWS // 2
PARTS = ((0, 768, (0, 1, 2)), (768, 768, (2, 0, 1)), (1536, 512, (1, 2, 0)))
CUTS = (32, 64, 96)
f32 = jnp.float32
bf16 = jnp.bfloat16


def mm(a, b, contract=((1,), (0,))):
    return lax.dot_general(a, b, (contract, ((), ())), preferred_element_type=f32)


def step_kernel(
    owner_ref, offset_ref, table_ref, w_ins_ref, w_outs_ref, w_ini_ref, w_outi_ref,
    loss_ref, asked, returned, summed,
    table_rows, w_in, w_out, requests, asked_scalars, stage, rows, fetched, pick, pick_t,
    pre_act, hidden, unit, norm, queries, items, expo, soft, part_sums,
    q_send, q_recv, k_send, k_recv, slots, inputs, grad_out, grad_pre, core_send, core_recv, half, sum1, recv1, recv2, recv3,
    load_sems, send_sems, recv_sems, ring_send, ring_recv,
):
    t = lax.axis_index("table")
    dp = lax.axis_index("dp")
    me = t * GROUP + dp
    core = lax.rem(t, 2)
    z = lax.div(dp, QUERY_PEERS)
    a = lax.rem(dp, QUERY_PEERS)
    x = lax.div(a, 2)
    y = lax.rem(a, 2) * 2 + lax.div(t, 2)
    coords = (x, y, z)

    def place(device):
        return (lax.div(device, GROUP), lax.rem(device, GROUP))

    def chip(coords, core):
        cx, cy, cz = coords
        return (lax.rem(cy, 2) * 2 + core, cz * QUERY_PEERS + cx * 2 + lax.div(cy, 2))

    def send(src, dst, s_sem, r_sem, device):
        pltpu.make_async_remote_copy(
            src, dst, s_sem, r_sem, device_id=device, device_id_type=MESH
        ).start()

    def wait(ref, sem):
        pltpu.make_async_copy(ref, ref, sem).wait()

    loads = [
        pltpu.make_async_copy(src, dst, load_sems.at[i])
        for i, (src, dst) in enumerate(
            [
                (table_ref, table_rows),
                (w_ins_ref, w_in.at[0]),
                (w_outs_ref, w_out.at[0]),
                (w_ini_ref, w_in.at[1]),
                (w_outi_ref, w_out.at[1]),
            ]
        )
    ]
    for load in loads:
        load.start()

    barrier = pltpu.get_barrier_semaphore()

    @pl.loop(1, SHARDS)
    def _(step):
        pl.semaphore_signal(
            barrier, inc=1, device_id=place(lax.rem(me + step, SHARDS)), device_id_type=MESH
        )

    lane = lax.broadcasted_iota(jnp.int32, (PAIRS, SHARDS), 1)
    row = lax.broadcasted_iota(jnp.int32, (PAIRS, SHARDS), 0)
    below = jnp.zeros((SHARDS - 8, PAIRS), jnp.int32)
    owner = jnp.concatenate([owner_ref[...], below], axis=0).T
    offset = jnp.concatenate([offset_ref[...], below], axis=0).T
    names = [(owner[:, k : k + 1] == lane).astype(jnp.int32) for k in range(8)]
    offsets = sum(names[k] * offset[:, k : k + 1] for k in range(8))
    named_q = sum(names[:4])
    named_k = sum(names[4:])
    named = named_q + named_k
    rank = named
    for shift in (1, 2, 4, 8, 16, 32, 64):
        rank = rank + jnp.where(row >= shift, pltpu.roll(rank, shift, 0), 0)
    rank = rank - named
    by_slot = [
        jnp.sum(jnp.where(rank == r, offsets, 0), axis=0, keepdims=True) for r in range(CAP)
    ] + [jnp.sum(named, axis=0, keepdims=True)]
    by_slot = jnp.concatenate(
        by_slot + [jnp.zeros((SHARDS - CAP - 1, SHARDS), jnp.int32)], axis=0
    )
    requests[...] = by_slot.T.reshape(SHARDS, 1, SHARDS)

    pl.semaphore_wait(barrier, SHARDS - 1)

    others = pl.ds(0, SHARDS - 1)
    asked[me] = requests[me]

    @pl.loop(1, SHARDS)
    def _(step):
        d = lax.rem(me + step, SHARDS)
        send(requests.at[d], asked.at[me], send_sems.at[0], recv_sems.at[0], place(d))

    wait(asked.at[others], recv_sems.at[0])
    spread = pltpu.make_async_copy(asked, asked_scalars, load_sems.at[5])
    spread.start()
    loads[0].wait()
    spread.wait()

    def lookup(d):
        for slot in range(CAP):
            stage[slot : slot + 1, :] = table_rows[pl.ds(asked_scalars[d, 0, slot], 1), :]
        return stage[...].astype(bf16)

    @pl.loop(1, SHARDS)
    def _(step):
        d = lax.rem(me + step, SHARDS)
        rows[d] = lookup(d)
        send(rows.at[d], fetched.at[me], send_sems.at[1], recv_sems.at[1], place(d))

    fetched[me] = lookup(me)

    cut = 512
    rank_b, named_qb, named_kb = (v.astype(f32).astype(bf16) for v in (rank, named_q, named_k))
    for c in range(SHARDS * CAP // cut):
        col = lax.broadcasted_iota(jnp.int32, (SHARDS, cut), 1) + c * cut
        dev = lax.broadcasted_iota(jnp.int32, (SHARDS, cut), 0)
        spread_b = (lax.div(col, CAP) == dev).astype(bf16)
        hit = mm(rank_b, spread_b) == lax.rem(col, CAP).astype(f32)
        pick[0:PAIRS, c * cut : (c + 1) * cut] = jnp.where(hit, mm(named_qb, spread_b), 0.0).astype(bf16)
        pick[PAIRS:, c * cut : (c + 1) * cut] = jnp.where(hit, mm(named_kb, spread_b), 0.0).astype(bf16)
        col = lax.broadcasted_iota(jnp.int32, (cut, SHARDS), 0) + c * cut
        dev = lax.broadcasted_iota(jnp.int32, (cut, SHARDS), 1)
        spread_b = (lax.div(col, CAP) == dev).astype(bf16)
        rhs_t = ((1,), (1,))
        hit = mm(spread_b, rank_b, rhs_t) == lax.rem(col, CAP).astype(f32)
        pick_t[c * cut : (c + 1) * cut, 0:PAIRS] = jnp.where(hit, mm(spread_b, named_qb, rhs_t), 0.0).astype(bf16)
        pick_t[c * cut : (c + 1) * cut, PAIRS:] = jnp.where(hit, mm(spread_b, named_kb, rhs_t), 0.0).astype(bf16)

    for load in loads[1:]:
        load.wait()
    wait(rows.at[others], recv_sems.at[1])
    inputs[...] = (
        mm(pick[...], fetched[...].reshape(SHARDS * CAP, WIDTH)).astype(bf16).reshape(2, PAIRS, WIDTH)
    )

    for i in range(2):
        pre = mm(inputs[i], w_in[i])
        pre_act[i] = pre
        hid = (pre * lax.logistic(pre)).astype(bf16)
        hidden[i] = hid
        out = mm(hid, w_out[i])
        out_norm = jnp.sqrt(jnp.sum(out * out, axis=-1, keepdims=True) + 1e-06)
        unit[i] = out / out_norm
        norm[i] = jnp.broadcast_to(out_norm, (PAIRS, WIDTH))
        if i == 0:
            queries[a] = unit[0].astype(bf16)
            for j in range(1, QUERY_PEERS):
                peer = (t, z * QUERY_PEERS + lax.rem(a + j, QUERY_PEERS))
                send(queries.at[a], queries.at[a], send_sems.at[2], recv_sems.at[2], peer)
        else:
            items[z] = unit[1].astype(bf16)
            for j in range(1, ITEM_PEERS):
                peer = (t, lax.rem(z + j, ITEM_PEERS) * QUERY_PEERS + a)
                send(items.at[z], items.at[z], send_sems.at[3], recv_sems.at[3], peer)
    query_unit = queries[a].astype(f32)
    item_unit = items[z].astype(f32)
    wait(items.at[pl.ds(0, ITEM_PEERS - 1)], recv_sems.at[3])
    wait(queries.at[pl.ds(0, QUERY_PEERS - 1)], recv_sems.at[2])

    all_items = items[...].reshape(BLOCK_K, WIDTH)
    sums = []
    for c in range(QUERY_PEERS):
        e = jnp.exp(SCALE * mm(all_items, queries[c], ((1,), (1,))))
        expo[:, c * PAIRS : (c + 1) * PAIRS] = e
        soft[:, c * PAIRS : (c + 1) * PAIRS] = e.astype(bf16)
        sums.append(jnp.sum(e, axis=0, keepdims=True))
    part_sums[a] = jnp.concatenate(sums, axis=0)
    for j in range(1, QUERY_PEERS):
        peer = (t, z * QUERY_PEERS + lax.rem(a + j, QUERY_PEERS))
        send(part_sums.at[a], part_sums.at[a], send_sems.at[4], recv_sems.at[4], peer)

    def part_q(c):
        block = soft[:, pl.ds(pl.multiple_of(c * PAIRS, PAIRS), PAIRS)]
        return mm(block, all_items, ((0,), (0,)))

    for j in range(1, QUERY_PEERS):
        c = lax.rem(a + j, QUERY_PEERS)
        q_send[j - 1] = part_q(c).astype(bf16)
        send(q_send.at[j - 1], q_recv.at[j - 1], send_sems.at[5], recv_sems.at[5], (t, z * QUERY_PEERS + c))
    grad_q = part_q(a)
    own_score = SCALE * jnp.sum(query_unit * item_unit, axis=1, keepdims=True)
    own_score = jnp.sum(jnp.where(lane == row, own_score, 0.0), axis=0, keepdims=True)

    wait(part_sums.at[pl.ds(0, QUERY_PEERS - 1)], recv_sems.at[4])
    total = part_sums[0]
    for c in range(1, QUERY_PEERS):
        total = total + part_sums[c]
    mine = lax.broadcasted_iota(jnp.int32, (QUERY_PEERS, PAIRS), 0) == a
    own_total = jnp.sum(jnp.where(mine, total, 0.0), axis=0, keepdims=True)
    loss_ref[...] = jnp.log(own_total) - own_score
    inverse = 1.0 / total
    own_inverse = jnp.sum(jnp.where(lane == row, 1.0 / own_total, 0.0), axis=1, keepdims=True)
    for c in range(QUERY_PEERS):
        at = slice(c * PAIRS, (c + 1) * PAIRS)
        soft[:, at] = (expo[:, at] * inverse[c : c + 1, :]).astype(bf16)

    def part_k(c):
        block = soft[pl.ds(pl.multiple_of(c * PAIRS, PAIRS), PAIRS), :]
        return mm(block, queries[...].reshape(BLOCK_Q, WIDTH))

    for j in range(1, ITEM_PEERS):
        c = lax.rem(z + j, ITEM_PEERS)
        k_send[j - 1] = part_k(c).astype(bf16)
        send(k_send.at[j - 1], k_recv.at[j - 1], send_sems.at[6], recv_sems.at[6], (t, c * QUERY_PEERS + a))
    grad_k = part_k(z) - query_unit
    wait(q_recv, recv_sems.at[5])
    for j in range(QUERY_PEERS - 1):
        grad_q = grad_q + q_recv[j].astype(f32)
    grad_q = grad_q * own_inverse - item_unit
    wait(k_recv, recv_sems.at[6])
    for j in range(ITEM_PEERS - 1):
        grad_k = grad_k + k_recv[j].astype(f32)

    grad_x = []
    for i, grad_unit in enumerate((SCALE * grad_q, SCALE * grad_k)):
        u = unit[i]
        g = ((grad_unit - u * jnp.sum(grad_unit * u, axis=-1, keepdims=True)) / norm[i]).astype(bf16)
        grad_hidden = mm(g, w_out[i], ((1,), (1,)))
        pre = pre_act[i]
        s = lax.logistic(pre)
        gp = (grad_hidden * s * (1.0 + pre * (1.0 - s))).astype(bf16)
        grad_out[i] = g
        grad_pre[i] = gp
        grad_x.append(mm(gp, w_in[i], ((1,), (1,))).astype(bf16))

    def tower_rows(i, block):
        at = slice(block % 4 * WIDTH, (block % 4 + 1) * WIDTH)
        if block < 4:
            return mm(inputs[i], grad_pre[i, :, at], ((0,), (0,)))
        return mm(hidden[i, :, at], grad_out[i], ((0,), (0,)))

    for p, (base, size, axes) in enumerate(PARTS):
        for r in range(base, base + size, WIDTH):
            core_send[r : r + WIDTH] = tower_rows(1 - core, r // WIDTH).astype(bf16)
        at = pl.ds(base, size)
        send(core_send.at[at], core_recv.at[at], ring_send.at[p, 0], ring_recv.at[p, 0], chip(coords, 1 - core))

    slots[...] = (
        mm(pick_t[...], jnp.concatenate(grad_x, axis=0)).astype(bf16).reshape(SHARDS, CAP, WIDTH)
    )

    def send_slots(first, last):
        @pl.loop(first, last)
        def _(step):
            d = lax.rem(me + step, SHARDS)
            send(slots.at[d], returned.at[me], send_sems.at[7], recv_sems.at[7], place(d))

    send_slots(1, CUTS[0])
    returned[me] = slots[me]

    def along(axis, j):
        moved = list(coords)
        moved[axis] = lax.rem(coords[axis] + j, 4)
        return moved[axis], chip(moved, core)

    def rows_at(start, size):
        return pl.ds(pl.multiple_of(start, 16), size)

    at1, at2 = 0, 0
    spans = []
    for base, size, _ in PARTS:
        spans.append((at1, at2))
        at1, at2 = at1 + size // 4, at2 + size // 16
    for p, (base, size, axes) in enumerate(PARTS):
        n = size // 4
        wait(core_recv.at[pl.ds(base, size)], ring_recv.at[p, 0])
        for r in range(base, base + size, WIDTH):
            at = slice(r, r + WIDTH)
            half[at] = (tower_rows(core, r // WIDTH) + core_recv[at].astype(f32)).astype(bf16)
        for j in range(1, 4):
            c, device = along(axes[0], j)
            send(half.at[rows_at(base + c * n, n)], recv1.at[j - 1, pl.ds(spans[p][0], n)],
                 ring_send.at[p, 1], ring_recv.at[p, 1], device)
    send_slots(CUTS[0], CUTS[1])
    for p, (base, size, axes) in enumerate(PARTS):
        n, m = size // 4, size // 16
        at = pl.ds(spans[p][0], n)
        wait(recv1.at[:, at], ring_recv.at[p, 1])
        total1 = half[rows_at(base + coords[axes[0]] * n, n)].astype(f32)
        for j in range(3):
            total1 = total1 + recv1[j, at].astype(f32)
        sum1[at] = total1.astype(bf16)
        for j in range(1, 4):
            c, device = along(axes[1], j)
            send(sum1.at[rows_at(spans[p][0] + c * m, m)], recv2.at[j - 1, pl.ds(spans[p][1], m)],
                 ring_send.at[p, 2], ring_recv.at[p, 2], device)
    send_slots(CUTS[1], CUTS[2])
    for p, (base, size, axes) in enumerate(PARTS):
        m = size // 16
        at = pl.ds(spans[p][1], m)
        wait(recv2.at[:, at], ring_recv.at[p, 2])
        total2 = sum1[rows_at(spans[p][0] + coords[axes[1]] * m, m)].astype(f32)
        for j in range(3):
            total2 = total2 + recv2[j, at].astype(f32)
        c3 = coords[axes[2]]
        recv3[c3, at] = total2.astype(bf16)
        for j in range(1, 4):
            _, device = along(axes[2], j)
            send(recv3.at[c3, at], recv3.at[c3, at], ring_send.at[p, 3], ring_recv.at[p, 3], device)
    send_slots(CUTS[2], SHARDS)
    for p, (base, size, axes) in enumerate(PARTS):
        n, m = size // 4, size // 16
        at = pl.ds(spans[p][1], m)
        wait(recv3.at[pl.ds(0, 3), at], ring_recv.at[p, 3])
        total3 = recv3[0, at].astype(f32)
        for j in range(1, 4):
            total3 = total3 + recv3[j, at].astype(f32)
        mine = rows_at(core * HALF + base + coords[axes[0]] * n + coords[axes[1]] * m, m)
        summed[mine] = total3.astype(bf16)
        for j in range(1, 4):
            _, device = along(axes[1], j)
            send(summed.at[mine], summed.at[mine], ring_send.at[p, 4], ring_recv.at[p, 4], device)
    for p, (base, size, axes) in enumerate(PARTS):
        n, m = size // 4, size // 16
        wait(summed.at[pl.ds(0, 3 * m)], ring_recv.at[p, 4])
        mine = rows_at(core * HALF + base + coords[axes[0]] * n, n)
        for j in range(1, 4):
            _, device = along(axes[0], j)
            send(summed.at[mine], summed.at[mine], ring_send.at[p, 4 + j], ring_recv.at[p, 4 + j], device)
        send(summed.at[mine], summed.at[mine], ring_send.at[p, 8], ring_recv.at[p, 8], chip(coords, 1 - core))
    for j in (1, 3, 2):
        for p, (base, size, axes) in enumerate(PARTS):
            n = size // 4
            wait(summed.at[pl.ds(0, n)], ring_recv.at[p, 4 + j])
            there = rows_at(core * HALF + base + lax.rem(coords[axes[0]] + 4 - j, 4) * n, n)
            send(summed.at[there], summed.at[there], ring_send.at[p, 8], ring_recv.at[p, 8], chip(coords, 1 - core))
    for p, (base, size, axes) in enumerate(PARTS):
        wait(summed.at[pl.ds(0, size)], ring_recv.at[p, 8])

    wait(rows.at[others], recv_sems.at[7])
    for ref, i in (
        (requests.at[others], 0),
        (rows.at[others], 1),
        (queries.at[pl.ds(0, QUERY_PEERS - 1)], 2),
        (items.at[pl.ds(0, ITEM_PEERS - 1)], 3),
        (part_sums.at[pl.ds(0, QUERY_PEERS - 1)], 4),
        (q_send, 5),
        (k_send, 6),
        (slots.at[others], 7),
    ):
        wait(ref, send_sems.at[i])
    for p, (base, size, axes) in enumerate(PARTS):
        n, m = size // 4, size // 16
        for i, count in enumerate((size, 3 * n, 3 * m, 3 * m, 3 * m, n, n, n, size)):
            wait(summed.at[pl.ds(0, count)], ring_send.at[p, i])


def train_step(owner, offset, table, query_in, query_out, item_in, item_out):
    rows1 = sum(size // 4 for _, size, _ in PARTS)
    rows2 = sum(size // 16 for _, size, _ in PARTS)
    vmem = pl.BlockSpec(memory_space=pltpu.VMEM)
    hbm = pl.BlockSpec(memory_space=pl.ANY)
    V = pltpu.VMEM
    return pl.pallas_call(
        step_kernel,
        out_shape=(
            jax.ShapeDtypeStruct((1, PAIRS), f32),
            jax.ShapeDtypeStruct((SHARDS, 1, SHARDS), jnp.int32),
            jax.ShapeDtypeStruct((SHARDS, CAP, WIDTH), bf16),
            jax.ShapeDtypeStruct((GRAD_ROWS, WIDTH), bf16),
        ),
        in_specs=[vmem, vmem, hbm, hbm, hbm, hbm, hbm],
        out_specs=(vmem,) * 4,
        scratch_shapes=[
            V((ROWS, WIDTH), f32),
            V((2, WIDTH, HIDDEN), bf16),
            V((2, HIDDEN, WIDTH), bf16),
            V((SHARDS, 1, SHARDS), jnp.int32),
            pltpu.SMEM((SHARDS, 1, SHARDS), jnp.int32),
            V((CAP, WIDTH), f32),
            V((SHARDS, CAP, WIDTH), bf16),
            V((SHARDS, CAP, WIDTH), bf16),
            V((2 * PAIRS, SHARDS * CAP), bf16),
            V((SHARDS * CAP, 2 * PAIRS), bf16),
            V((2, PAIRS, HIDDEN), f32),
            V((2, PAIRS, HIDDEN), bf16),
            V((2, PAIRS, WIDTH), f32),
            V((2, PAIRS, WIDTH), f32),
            V((QUERY_PEERS, PAIRS, WIDTH), bf16),
            V((ITEM_PEERS, PAIRS, WIDTH), bf16),
            V((BLOCK_K, BLOCK_Q), f32),
            V((BLOCK_K, BLOCK_Q), bf16),
            V((QUERY_PEERS, QUERY_PEERS, PAIRS), f32),
            V((QUERY_PEERS - 1, PAIRS, WIDTH), bf16),
            V((QUERY_PEERS - 1, PAIRS, WIDTH), bf16),
            V((ITEM_PEERS - 1, PAIRS, WIDTH), bf16),
            V((ITEM_PEERS - 1, PAIRS, WIDTH), bf16),
            V((SHARDS, CAP, WIDTH), bf16),
            V((2, PAIRS, WIDTH), bf16),
            V((2, PAIRS, WIDTH), bf16),
            V((2, PAIRS, HIDDEN), bf16),
            V((HALF, WIDTH), bf16),
            V((HALF, WIDTH), bf16),
            V((HALF, WIDTH), bf16),
            V((rows1, WIDTH), bf16),
            V((3, rows1, WIDTH), bf16),
            V((3, rows2, WIDTH), bf16),
            V((4, rows2, WIDTH), bf16),
            pltpu.SemaphoreType.DMA((6,)),
            pltpu.SemaphoreType.DMA((8,)),
            pltpu.SemaphoreType.DMA((8,)),
            pltpu.SemaphoreType.DMA((len(PARTS), 9)),
            pltpu.SemaphoreType.DMA((len(PARTS), 9)),
        ],
        compiler_params=pltpu.CompilerParams(
            collective_id=0, has_side_effects=True, vmem_limit_bytes=56 << 20
        ),
    )(owner, offset, table, query_in, query_out, item_in, item_out)


def update_kernel(
    asked_ref, returned_ref, summed_ref, loss_ref,
    table_grad, q_in, q_out, k_in, k_out, loss_out,
    asked, returned, summed, total, other, wide_in, wide_out, stage, sems,
):
    loads = [
        pltpu.make_async_copy(src, dst, sems.at[i])
        for i, (src, dst) in enumerate(
            [(summed_ref, summed), (asked_ref, asked), (returned_ref, returned)]
        )
    ]
    for load in loads:
        load.start()
    loss_out[...] = loss_ref[...]

    @pl.loop(0, ROWS, step=256)
    def _(r):
        total[pl.ds(r, 256), :] = jnp.zeros((256, WIDTH), f32)
        other[pl.ds(r, 256), :] = jnp.zeros((256, WIDTH), f32)

    loads[0].wait()
    copies = []
    for i, (out_in, out_out) in enumerate(((q_in, q_out), (k_in, k_out))):
        base = i * HALF
        for c in range(0, HIDDEN, WIDTH):
            wide_in[i, :, c : c + WIDTH] = summed[base + c : base + c + WIDTH].astype(f32)
        wide_out[i] = summed[base + HIDDEN : base + HALF].astype(f32)
        copies.append(pltpu.make_async_copy(wide_in.at[i], out_in, sems.at[3 + 2 * i]))
        copies.append(pltpu.make_async_copy(wide_out.at[i], out_out, sems.at[4 + 2 * i]))
        copies[-2].start()
        copies[-1].start()
    loads[1].wait()
    loads[2].wait()

    @pl.loop(0, SHARDS)
    def _(d):
        stage[...] = returned[d].astype(f32)
        count = asked[d, 0, CAP]
        for first in range(0, CAP, 4):

            @pl.when(count > first)
            def _():
                for slot in range(first, first + 4, 2):
                    at = pl.ds(asked[d, 0, slot], 1)
                    at2 = pl.ds(asked[d, 0, slot + 1], 1)
                    total[at, :] += stage[slot : slot + 1, :]
                    other[at2, :] += stage[slot + 1 : slot + 2, :]

    cut = ROWS // 8
    for r in range(0, ROWS, cut):

        @pl.loop(r, r + cut, step=128)
        def _(q):
            total[pl.ds(q, 128), :] += other[pl.ds(q, 128), :]

        at = pl.ds(r, cut)
        copies.append(pltpu.make_async_copy(total.at[at], table_grad.at[at], sems.at[7 + r // cut]))
        copies[-1].start()
    for copy in copies:
        copy.wait()


def update(asked, returned, summed, loss):
    vmem = pl.BlockSpec(memory_space=pltpu.VMEM)
    hbm = pl.BlockSpec(memory_space=pl.ANY)
    in_shape = jax.ShapeDtypeStruct((WIDTH, HIDDEN), f32)
    out_shape = jax.ShapeDtypeStruct((HIDDEN, WIDTH), f32)
    table_shape = jax.ShapeDtypeStruct((ROWS, WIDTH), f32)
    loss_shape = jax.ShapeDtypeStruct((1, PAIRS), f32)
    return pl.pallas_call(
        update_kernel,
        out_shape=(table_shape, in_shape, out_shape, in_shape, out_shape, loss_shape),
        in_specs=[hbm, hbm, hbm, vmem],
        out_specs=(hbm,) * 5 + (vmem,),
        scratch_shapes=[
            pltpu.SMEM((SHARDS, 1, SHARDS), jnp.int32),
            pltpu.VMEM((SHARDS, CAP, WIDTH), bf16),
            pltpu.VMEM((GRAD_ROWS, WIDTH), bf16),
            pltpu.VMEM((ROWS, WIDTH), f32),
            pltpu.VMEM((ROWS, WIDTH), f32),
            pltpu.VMEM((2, WIDTH, HIDDEN), f32),
            pltpu.VMEM((2, HIDDEN, WIDTH), f32),
            pltpu.VMEM((CAP, WIDTH), f32),
            pltpu.SemaphoreType.DMA((15,)),
        ],
        compiler_params=pltpu.CompilerParams(vmem_limit_bytes=56 << 20),
    )(asked, returned, summed, loss)


def local(table, feature_owner, feature_offset, query_in, query_out, item_in, item_out):
    loss, asked, returned, summed = train_step(
        feature_owner.T, feature_offset.T, table, query_in, query_out, item_in, item_out
    )
    table_grad, q_in, q_out, k_in, k_out, loss = update(asked, returned, summed, loss)
    return (loss.reshape(PAIRS), table_grad, q_in, q_out, k_in, k_out)


def solution(mesh):
    in_specs = (
        P(("table", "dp"), None),
        P(("table", "dp"), None),
        P(("table", "dp"), None),
        P(),
        P(),
        P(),
        P(),
    )
    out_specs = (P(("table", "dp")), P(("table", "dp"), None), P(), P(), P(), P())
    return jax.shard_map(local, mesh=mesh, in_specs=in_specs, out_specs=out_specs, check_vma=False)
```

```python
import jax
import jax.numpy as jnp
from jax import lax
from jax.experimental import pallas as pl
from jax.experimental.pallas import tpu as pltpu
from jax.sharding import PartitionSpec as P

MESH = pl.DeviceIdType.MESH
SCALE = 20.0
SHARDS = 128
GROUP = 32
CAP = 16
PAIRS = 128
WIDTH = 256
HIDDEN = 1024
ROWS = 8192
QUERY_PEERS = 8
ITEM_PEERS = 4
BLOCK_Q = QUERY_PEERS * PAIRS
BLOCK_K = ITEM_PEERS * PAIRS
GRAD_ROWS = 4 * HIDDEN
HALF = GRAD_ROWS // 2
SHARE = HALF // 2
PARTS = (
    ((0, 256, (0, 1, 2)), (256, 256, (1, 2, 0)), (512, 512, (2, 0, 1))),
    ((0, 512, (0, 1, 2)), (512, 256, (1, 2, 0)), (768, 256, (2, 0, 1))),
)
N_PARTS = 6
ID_RUNS = ((1, 32), (32, 64), (64, 96), (96, 128))
CUTS = (32, 64, 96)
f32 = jnp.float32
bf16 = jnp.bfloat16


def mm(a, b, contract=((1,), (0,))):
    return lax.dot_general(a, b, (contract, ((), ())), preferred_element_type=f32)


def step_kernel(
    owner_ref, offset_ref, table_ref, w_ins_ref, w_outs_ref, w_ini_ref, w_outi_ref,
    loss_ref, asked, returned, summed,
    table_rows, w_in, w_out, requests, asked_scalars, stage, rows, fetched, pick, pick_t,
    pre_act, hidden, unit, norm, queries, items, expo, soft, part_sums,
    q_send, q_recv, k_send, k_recv, slots, inputs, grad_out, grad_pre, core_send, core_recv, half, sum1, recv1, recv2, recv3,
    load_sems, id_recv, send_sems, recv_sems, ring_send, ring_recv,
):
    t = lax.axis_index("table")
    dp = lax.axis_index("dp")
    me = t * GROUP + dp
    core = lax.rem(t, 2)
    z = lax.div(dp, QUERY_PEERS)
    a = lax.rem(dp, QUERY_PEERS)
    x = lax.div(a, 2)
    y = lax.rem(a, 2) * 2 + lax.div(t, 2)
    coords = (x, y, z)

    def place(device):
        return (lax.div(device, GROUP), lax.rem(device, GROUP))

    def chip(coords, core):
        cx, cy, cz = coords
        return (lax.rem(cy, 2) * 2 + core, cz * QUERY_PEERS + cx * 2 + lax.div(cy, 2))

    def send(src, dst, s_sem, r_sem, device):
        pltpu.make_async_remote_copy(
            src, dst, s_sem, r_sem, device_id=device, device_id_type=MESH
        ).start()

    def wait(ref, sem):
        pltpu.make_async_copy(ref, ref, sem).wait()

    loads = [
        pltpu.make_async_copy(src, dst, load_sems.at[i])
        for i, (src, dst) in enumerate(
            [
                (table_ref, table_rows),
                (w_ins_ref, w_in.at[0]),
                (w_outs_ref, w_out.at[0]),
                (w_ini_ref, w_in.at[1]),
                (w_outi_ref, w_out.at[1]),
            ]
        )
    ]
    for load in loads:
        load.start()

    barrier = pltpu.get_barrier_semaphore()

    @pl.loop(1, SHARDS, unroll=4)
    def _(step):
        pl.semaphore_signal(
            barrier, inc=1, device_id=place(lax.rem(me + step, SHARDS)), device_id_type=MESH
        )

    lane = lax.broadcasted_iota(jnp.int32, (PAIRS, SHARDS), 1)
    row = lax.broadcasted_iota(jnp.int32, (PAIRS, SHARDS), 0)
    below = jnp.zeros((SHARDS - 8, PAIRS), jnp.int32)
    owner = jnp.concatenate([owner_ref[...], below], axis=0).T
    offset = jnp.concatenate([offset_ref[...], below], axis=0).T
    names = [(owner[:, k : k + 1] == lane).astype(jnp.int32) for k in range(8)]
    offsets = sum(names[k] * offset[:, k : k + 1] for k in range(8))
    named_q = sum(names[:4])
    named_k = sum(names[4:])
    named = named_q + named_k
    rank = named
    for shift in (1, 2, 4, 8, 16, 32, 64):
        rank = rank + jnp.where(row >= shift, pltpu.roll(rank, shift, 0), 0)
    rank = rank - named
    by_slot = [
        jnp.sum(jnp.where(rank == r, offsets, 0), axis=0, keepdims=True) for r in range(CAP)
    ] + [jnp.sum(named, axis=0, keepdims=True)]
    by_slot = jnp.concatenate(
        by_slot + [jnp.zeros((SHARDS - CAP - 1, SHARDS), jnp.int32)], axis=0
    )
    requests[...] = by_slot.T.reshape(SHARDS, 1, SHARDS)

    pl.semaphore_wait(barrier, SHARDS - 1)

    others = pl.ds(0, SHARDS - 1)
    asked[0] = requests[me]
    for run, (first, last) in enumerate(ID_RUNS):

        @pl.loop(first, last)
        def _(step):
            d = lax.rem(me + step, SHARDS)
            send(requests.at[d], asked.at[step], send_sems.at[0], id_recv.at[run], place(d))

    def lookup(step):
        for slot in range(CAP):
            stage[slot : slot + 1, :] = table_rows[pl.ds(asked_scalars[step, 0, slot], 1), :]
        return stage[...].astype(bf16)

    def send_rows(first, last):
        @pl.loop(first, last)
        def _(step):
            rows[step] = lookup(step)
            d = lax.rem(me + SHARDS - step, SHARDS)
            send(rows.at[step], fetched.at[me], send_sems.at[1], recv_sems.at[1], place(d))

    for run, (first, last) in enumerate(ID_RUNS):
        wait(asked.at[pl.ds(first, last - first)], id_recv.at[run])
        at = pl.ds(first if run else 0, last - first if run else last)
        spread = pltpu.make_async_copy(asked.at[at], asked_scalars.at[at], load_sems.at[5])
        spread.start()
        if run == 0:
            loads[0].wait()
        else:
            send_rows(*ID_RUNS[run - 1])
        spread.wait()
    send_rows(*ID_RUNS[-1])
    fetched[me] = lookup(0)

    cut = 512
    rank_b, named_qb, named_kb = (v.astype(f32).astype(bf16) for v in (rank, named_q, named_k))
    for c in range(SHARDS * CAP // cut):
        col = lax.broadcasted_iota(jnp.int32, (SHARDS, cut), 1) + c * cut
        dev = lax.broadcasted_iota(jnp.int32, (SHARDS, cut), 0)
        spread_b = (lax.div(col, CAP) == dev).astype(bf16)
        hit = mm(rank_b, spread_b) == lax.rem(col, CAP).astype(f32)
        pick[0:PAIRS, c * cut : (c + 1) * cut] = jnp.where(hit, mm(named_qb, spread_b), 0.0).astype(bf16)
        pick[PAIRS:, c * cut : (c + 1) * cut] = jnp.where(hit, mm(named_kb, spread_b), 0.0).astype(bf16)
        col = lax.broadcasted_iota(jnp.int32, (cut, SHARDS), 0) + c * cut
        dev = lax.broadcasted_iota(jnp.int32, (cut, SHARDS), 1)
        spread_b = (lax.div(col, CAP) == dev).astype(bf16)
        rhs_t = ((1,), (1,))
        hit = mm(spread_b, rank_b, rhs_t) == lax.rem(col, CAP).astype(f32)
        pick_t[c * cut : (c + 1) * cut, 0:PAIRS] = jnp.where(hit, mm(spread_b, named_qb, rhs_t), 0.0).astype(bf16)
        pick_t[c * cut : (c + 1) * cut, PAIRS:] = jnp.where(hit, mm(spread_b, named_kb, rhs_t), 0.0).astype(bf16)

    for load in loads[1:]:
        load.wait()
    wait(rows.at[others], recv_sems.at[1])
    inputs[...] = (
        mm(pick[...], fetched[...].reshape(SHARDS * CAP, WIDTH)).astype(bf16).reshape(2, PAIRS, WIDTH)
    )

    for i in range(2):
        pre = mm(inputs[i], w_in[i])
        pre_act[i] = pre
        hid = (pre * lax.logistic(pre)).astype(bf16)
        hidden[i] = hid
        out = mm(hid, w_out[i])
        out_norm = jnp.sqrt(jnp.sum(out * out, axis=-1, keepdims=True) + 1e-06)
        unit[i] = out / out_norm
        norm[i] = jnp.broadcast_to(out_norm, (PAIRS, WIDTH))
        if i == 0:
            queries[a] = unit[0].astype(bf16)
            for j in range(1, QUERY_PEERS):
                peer = (t, z * QUERY_PEERS + lax.rem(a + j, QUERY_PEERS))
                send(queries.at[a], queries.at[a], send_sems.at[2], recv_sems.at[2], peer)
        else:
            items[z] = unit[1].astype(bf16)
            for j in range(1, ITEM_PEERS):
                peer = (t, lax.rem(z + j, ITEM_PEERS) * QUERY_PEERS + a)
                send(items.at[z], items.at[z], send_sems.at[3], recv_sems.at[3], peer)
    query_unit = queries[a].astype(f32)
    item_unit = items[z].astype(f32)
    wait(items.at[pl.ds(0, ITEM_PEERS - 1)], recv_sems.at[3])
    wait(queries.at[pl.ds(0, QUERY_PEERS - 1)], recv_sems.at[2])

    all_items = items[...].reshape(BLOCK_K, WIDTH)
    sums = []
    for c in range(QUERY_PEERS):
        e = jnp.exp(SCALE * mm(all_items, queries[c], ((1,), (1,))))
        expo[:, c * PAIRS : (c + 1) * PAIRS] = e
        soft[:, c * PAIRS : (c + 1) * PAIRS] = e.astype(bf16)
        sums.append(jnp.sum(e, axis=0, keepdims=True))
    part_sums[a] = jnp.concatenate(sums, axis=0)
    for j in range(1, QUERY_PEERS):
        peer = (t, z * QUERY_PEERS + lax.rem(a + j, QUERY_PEERS))
        send(part_sums.at[a], part_sums.at[a], send_sems.at[4], recv_sems.at[4], peer)

    def part_q(c):
        block = soft[:, pl.ds(pl.multiple_of(c * PAIRS, PAIRS), PAIRS)]
        return mm(block, all_items, ((0,), (0,)))

    for j in range(1, QUERY_PEERS):
        c = lax.rem(a + j, QUERY_PEERS)
        q_send[j - 1] = part_q(c).astype(bf16)
        send(q_send.at[j - 1], q_recv.at[j - 1], send_sems.at[5], recv_sems.at[5], (t, z * QUERY_PEERS + c))
    grad_q = part_q(a)
    own_score = SCALE * jnp.sum(query_unit * item_unit, axis=1, keepdims=True)
    own_score = jnp.sum(jnp.where(lane == row, own_score, 0.0), axis=0, keepdims=True)

    wait(part_sums.at[pl.ds(0, QUERY_PEERS - 1)], recv_sems.at[4])
    total = part_sums[0]
    for c in range(1, QUERY_PEERS):
        total = total + part_sums[c]
    mine = lax.broadcasted_iota(jnp.int32, (QUERY_PEERS, PAIRS), 0) == a
    own_total = jnp.sum(jnp.where(mine, total, 0.0), axis=0, keepdims=True)
    loss_ref[...] = jnp.log(own_total) - own_score
    inverse = 1.0 / total
    own_inverse = jnp.sum(jnp.where(lane == row, 1.0 / own_total, 0.0), axis=1, keepdims=True)
    for c in range(QUERY_PEERS):
        at = slice(c * PAIRS, (c + 1) * PAIRS)
        soft[:, at] = (expo[:, at] * inverse[c : c + 1, :]).astype(bf16)

    def part_k(c):
        block = soft[pl.ds(pl.multiple_of(c * PAIRS, PAIRS), PAIRS), :]
        return mm(block, queries[...].reshape(BLOCK_Q, WIDTH))

    for j in range(1, ITEM_PEERS):
        c = lax.rem(z + j, ITEM_PEERS)
        k_send[j - 1] = part_k(c).astype(bf16)
        send(k_send.at[j - 1], k_recv.at[j - 1], send_sems.at[6], recv_sems.at[6], (t, c * QUERY_PEERS + a))
    grad_k = part_k(z) - query_unit

    def back(i, grad_unit):
        u = unit[i]
        g = ((grad_unit - u * jnp.sum(grad_unit * u, axis=-1, keepdims=True)) / norm[i]).astype(bf16)
        grad_hidden = mm(g, w_out[i], ((1,), (1,)))
        pre = pre_act[i]
        s = lax.logistic(pre)
        gp = (grad_hidden * s * (1.0 + pre * (1.0 - s))).astype(bf16)
        grad_out[i] = g
        grad_pre[i] = gp

    def share_rows(i, c, block):
        at = pl.ds(pl.multiple_of((c * 2 + block % 2) * WIDTH, WIDTH), WIDTH)
        if block < 2:
            return mm(inputs[i], grad_pre[i, :, at], ((0,), (0,)))
        return mm(hidden[i, :, at], grad_out[i], ((0,), (0,)))

    def along(axis, j):
        moved = list(coords)
        moved[axis] = lax.rem(coords[axis] + j, 4)
        return moved[axis], chip(moved, core)

    def rows_at(start, size):
        return pl.ds(pl.multiple_of(start, 16), size)

    parts = ([], [])
    at1, at2 = 0, 0
    for i in range(2):
        for base, size, axes in PARTS[i]:
            parts[i].append((len(parts[0]) + len(parts[1]), i * SHARE + base, size, axes, at1, at2))
            at1, at2 = at1 + size // 4, at2 + size // 16

    def final(i, base):
        return i * HALF + core * SHARE + base - i * SHARE

    def give_core(i):
        for p, base, size, axes, at1, at2 in parts[i]:
            for r in range(base, base + size, WIDTH):
                block = (r - i * SHARE) // WIDTH
                core_send[r : r + WIDTH] = share_rows(i, 1 - core, block).astype(bf16)
            at = pl.ds(base, size)
            send(core_send.at[at], core_recv.at[at], ring_send.at[p, 0], ring_recv.at[p, 0], chip(coords, 1 - core))

    def step1(i):
        for p, base, size, axes, at1, at2 in parts[i]:
            n = size // 4
            own = [share_rows(i, core, (r - i * SHARE) // WIDTH) for r in range(base, base + size, WIDTH)]
            wait(core_recv.at[pl.ds(base, size)], ring_recv.at[p, 0])
            for k, r in enumerate(range(base, base + size, WIDTH)):
                half[r : r + WIDTH] = (own[k] + core_recv[r : r + WIDTH].astype(f32)).astype(bf16)
            for j in range(1, 4):
                c, device = along(axes[0], j)
                send(half.at[rows_at(base + c * n, n)], recv1.at[j - 1, pl.ds(at1, n)],
                     ring_send.at[p, 1], ring_recv.at[p, 1], device)

    def step2(i):
        for p, base, size, axes, at1, at2 in parts[i]:
            n, m = size // 4, size // 16
            at = pl.ds(at1, n)
            wait(recv1.at[:, at], ring_recv.at[p, 1])
            total1 = half[rows_at(base + coords[axes[0]] * n, n)].astype(f32)
            for j in range(3):
                total1 = total1 + recv1[j, at].astype(f32)
            sum1[at] = total1.astype(bf16)
            for j in range(1, 4):
                c, device = along(axes[1], j)
                send(sum1.at[rows_at(at1 + c * m, m)], recv2.at[j - 1, pl.ds(at2, m)],
                     ring_send.at[p, 2], ring_recv.at[p, 2], device)

    def step3(i):
        for p, base, size, axes, at1, at2 in parts[i]:
            m = size // 16
            at = pl.ds(at2, m)
            wait(recv2.at[:, at], ring_recv.at[p, 2])
            total2 = sum1[rows_at(at1 + coords[axes[1]] * m, m)].astype(f32)
            for j in range(3):
                total2 = total2 + recv2[j, at].astype(f32)
            c3 = coords[axes[2]]
            recv3[c3, at] = total2.astype(bf16)
            for j in range(1, 4):
                _, device = along(axes[2], j)
                send(recv3.at[c3, at], recv3.at[c3, at], ring_send.at[p, 3], ring_recv.at[p, 3], device)

    def step4(i):
        for p, base, size, axes, at1, at2 in parts[i]:
            n, m = size // 4, size // 16
            at = pl.ds(at2, m)
            wait(recv3.at[pl.ds(0, 3), at], ring_recv.at[p, 3])
            total3 = recv3[0, at].astype(f32)
            for j in range(1, 4):
                total3 = total3 + recv3[j, at].astype(f32)
            mine = rows_at(final(i, base) + coords[axes[0]] * n + coords[axes[1]] * m, m)
            summed[mine] = total3.astype(bf16)
            for j in range(1, 4):
                _, device = along(axes[1], j)
                send(summed.at[mine], summed.at[mine], ring_send.at[p, 4], ring_recv.at[p, 4], device)

    def step5(i):
        for p, base, size, axes, at1, at2 in parts[i]:
            n, m = size // 4, size // 16
            wait(summed.at[pl.ds(0, 3 * m)], ring_recv.at[p, 4])
            mine = rows_at(final(i, base) + coords[axes[0]] * n, n)
            for j in range(1, 4):
                _, device = along(axes[0], j)
                send(summed.at[mine], summed.at[mine], ring_send.at[p, 4 + j], ring_recv.at[p, 4 + j], device)
            send(summed.at[mine], summed.at[mine], ring_send.at[p, 8], ring_recv.at[p, 8], chip(coords, 1 - core))

    def step6(i):
        for j in (1, 3, 2):
            for p, base, size, axes, at1, at2 in parts[i]:
                n = size // 4
                wait(summed.at[pl.ds(0, n)], ring_recv.at[p, 4 + j])
                there = rows_at(final(i, base) + lax.rem(coords[axes[0]] + 4 - j, 4) * n, n)
                send(summed.at[there], summed.at[there], ring_send.at[p, 8], ring_recv.at[p, 8], chip(coords, 1 - core))

    def send_slots(first, last):
        @pl.loop(first, last)
        def _(step):
            d = lax.rem(me + step, SHARDS)
            send(slots.at[d], returned.at[step], send_sems.at[7], recv_sems.at[7], place(d))

    wait(q_recv, recv_sems.at[5])
    for j in range(QUERY_PEERS - 1):
        grad_q = grad_q + q_recv[j].astype(f32)
    back(0, SCALE * (grad_q * own_inverse - item_unit))
    give_core(0)
    step1(0)
    wait(k_recv, recv_sems.at[6])
    for j in range(ITEM_PEERS - 1):
        grad_k = grad_k + k_recv[j].astype(f32)
    back(1, SCALE * grad_k)
    give_core(1)

    grad_x = [mm(grad_pre[i], w_in[i], ((1,), (1,))).astype(bf16) for i in range(2)]
    slots[...] = (
        mm(pick_t[...], jnp.concatenate(grad_x, axis=0)).astype(bf16).reshape(SHARDS, CAP, WIDTH)
    )
    send_slots(1, CUTS[0])
    returned[0] = slots[me]
    step1(1)
    step2(0)
    send_slots(CUTS[0], CUTS[1])
    step2(1)
    step3(0)
    send_slots(CUTS[1], CUTS[2])
    step3(1)
    step4(0)
    send_slots(CUTS[2], SHARDS)
    step4(1)
    step5(0)
    step5(1)
    step6(0)
    step6(1)
    for p, base, size, axes, at1, at2 in parts[0] + parts[1]:
        wait(summed.at[pl.ds(0, size)], ring_recv.at[p, 8])

    wait(rows.at[others], recv_sems.at[7])
    for ref, i in (
        (requests.at[others], 0),
        (rows.at[others], 1),
        (queries.at[pl.ds(0, QUERY_PEERS - 1)], 2),
        (items.at[pl.ds(0, ITEM_PEERS - 1)], 3),
        (part_sums.at[pl.ds(0, QUERY_PEERS - 1)], 4),
        (q_send, 5),
        (k_send, 6),
        (slots.at[others], 7),
    ):
        wait(ref, send_sems.at[i])
    for p, base, size, axes, at1, at2 in parts[0] + parts[1]:
        n, m = size // 4, size // 16
        for i, count in enumerate((size, 3 * n, 3 * m, 3 * m, 3 * m, n, n, n, size)):
            wait(summed.at[pl.ds(0, count)], ring_send.at[p, i])


def train_step(owner, offset, table, query_in, query_out, item_in, item_out):
    rows1, rows2 = HALF // 4, HALF // 16
    vmem = pl.BlockSpec(memory_space=pltpu.VMEM)
    hbm = pl.BlockSpec(memory_space=pl.ANY)
    V = pltpu.VMEM
    return pl.pallas_call(
        step_kernel,
        out_shape=(
            jax.ShapeDtypeStruct((1, PAIRS), f32),
            jax.ShapeDtypeStruct((SHARDS, 1, SHARDS), jnp.int32),
            jax.ShapeDtypeStruct((SHARDS, CAP, WIDTH), bf16),
            jax.ShapeDtypeStruct((GRAD_ROWS, WIDTH), bf16),
        ),
        in_specs=[vmem, vmem, hbm, hbm, hbm, hbm, hbm],
        out_specs=(vmem,) * 4,
        scratch_shapes=[
            V((ROWS, WIDTH), f32),
            V((2, WIDTH, HIDDEN), bf16),
            V((2, HIDDEN, WIDTH), bf16),
            V((SHARDS, 1, SHARDS), jnp.int32),
            pltpu.SMEM((SHARDS, 1, SHARDS), jnp.int32),
            V((CAP, WIDTH), f32),
            V((SHARDS, CAP, WIDTH), bf16),
            V((SHARDS, CAP, WIDTH), bf16),
            V((2 * PAIRS, SHARDS * CAP), bf16),
            V((SHARDS * CAP, 2 * PAIRS), bf16),
            V((2, PAIRS, HIDDEN), f32),
            V((2, PAIRS, HIDDEN), bf16),
            V((2, PAIRS, WIDTH), f32),
            V((2, PAIRS, WIDTH), f32),
            V((QUERY_PEERS, PAIRS, WIDTH), bf16),
            V((ITEM_PEERS, PAIRS, WIDTH), bf16),
            V((BLOCK_K, BLOCK_Q), f32),
            V((BLOCK_K, BLOCK_Q), bf16),
            V((QUERY_PEERS, QUERY_PEERS, PAIRS), f32),
            V((QUERY_PEERS - 1, PAIRS, WIDTH), bf16),
            V((QUERY_PEERS - 1, PAIRS, WIDTH), bf16),
            V((ITEM_PEERS - 1, PAIRS, WIDTH), bf16),
            V((ITEM_PEERS - 1, PAIRS, WIDTH), bf16),
            V((SHARDS, CAP, WIDTH), bf16),
            V((2, PAIRS, WIDTH), bf16),
            V((2, PAIRS, WIDTH), bf16),
            V((2, PAIRS, HIDDEN), bf16),
            V((HALF, WIDTH), bf16),
            V((HALF, WIDTH), bf16),
            V((HALF, WIDTH), bf16),
            V((rows1, WIDTH), bf16),
            V((3, rows1, WIDTH), bf16),
            V((3, rows2, WIDTH), bf16),
            V((4, rows2, WIDTH), bf16),
            pltpu.SemaphoreType.DMA((6,)),
            pltpu.SemaphoreType.DMA((len(ID_RUNS),)),
            pltpu.SemaphoreType.DMA((8,)),
            pltpu.SemaphoreType.DMA((8,)),
            pltpu.SemaphoreType.DMA((N_PARTS, 9)),
            pltpu.SemaphoreType.DMA((N_PARTS, 9)),
        ],
        compiler_params=pltpu.CompilerParams(
            collective_id=0, has_side_effects=True, vmem_limit_bytes=56 << 20
        ),
    )(owner, offset, table, query_in, query_out, item_in, item_out)


def update_kernel(
    asked_ref, returned_ref, summed_ref, loss_ref,
    table_grad, q_in, q_out, k_in, k_out, loss_out,
    asked, returned, summed, total, other, wide_in, wide_out, stage, sems,
):
    loads = [
        pltpu.make_async_copy(src, dst, sems.at[i])
        for i, (src, dst) in enumerate(
            [(summed_ref, summed), (asked_ref, asked), (returned_ref, returned)]
        )
    ]
    for load in loads:
        load.start()
    loss_out[...] = loss_ref[...]

    @pl.loop(0, ROWS, step=256)
    def _(r):
        total[pl.ds(r, 256), :] = jnp.zeros((256, WIDTH), f32)
        other[pl.ds(r, 256), :] = jnp.zeros((256, WIDTH), f32)

    loads[0].wait()
    copies = []
    for i, (out_in, out_out) in enumerate(((q_in, q_out), (k_in, k_out))):
        base = i * HALF
        for c in range(0, HIDDEN, WIDTH):
            at = base + c // (2 * WIDTH) * SHARE + c % (2 * WIDTH)
            wide_in[i, :, c : c + WIDTH] = summed[at : at + WIDTH].astype(f32)
            at += 2 * WIDTH
            wide_out[i, c : c + WIDTH] = summed[at : at + WIDTH].astype(f32)
        copies.append(pltpu.make_async_copy(wide_in.at[i], out_in, sems.at[3 + 2 * i]))
        copies.append(pltpu.make_async_copy(wide_out.at[i], out_out, sems.at[4 + 2 * i]))
        copies[-2].start()
        copies[-1].start()
    loads[1].wait()
    loads[2].wait()

    @pl.loop(0, SHARDS)
    def _(d):
        stage[...] = returned[d].astype(f32)
        count = asked[d, 0, CAP]
        for first in range(0, CAP, 4):

            @pl.when(count > first)
            def _():
                for slot in range(first, first + 4, 2):
                    at = pl.ds(asked[d, 0, slot], 1)
                    at2 = pl.ds(asked[d, 0, slot + 1], 1)
                    total[at, :] += stage[slot : slot + 1, :]
                    other[at2, :] += stage[slot + 1 : slot + 2, :]

    cut = ROWS // 8
    for r in range(0, ROWS, cut):

        @pl.loop(r, r + cut, step=128)
        def _(q):
            total[pl.ds(q, 128), :] += other[pl.ds(q, 128), :]

        at = pl.ds(r, cut)
        copies.append(pltpu.make_async_copy(total.at[at], table_grad.at[at], sems.at[7 + r // cut]))
        copies[-1].start()
    for copy in copies:
        copy.wait()


def update(asked, returned, summed, loss):
    vmem = pl.BlockSpec(memory_space=pltpu.VMEM)
    hbm = pl.BlockSpec(memory_space=pl.ANY)
    in_shape = jax.ShapeDtypeStruct((WIDTH, HIDDEN), f32)
    out_shape = jax.ShapeDtypeStruct((HIDDEN, WIDTH), f32)
    table_shape = jax.ShapeDtypeStruct((ROWS, WIDTH), f32)
    loss_shape = jax.ShapeDtypeStruct((1, PAIRS), f32)
    return pl.pallas_call(
        update_kernel,
        out_shape=(table_shape, in_shape, out_shape, in_shape, out_shape, loss_shape),
        in_specs=[hbm, hbm, hbm, vmem],
        out_specs=(hbm,) * 5 + (vmem,),
        scratch_shapes=[
            pltpu.SMEM((SHARDS, 1, SHARDS), jnp.int32),
            pltpu.VMEM((SHARDS, CAP, WIDTH), bf16),
            pltpu.VMEM((GRAD_ROWS, WIDTH), bf16),
            pltpu.VMEM((ROWS, WIDTH), f32),
            pltpu.VMEM((ROWS, WIDTH), f32),
            pltpu.VMEM((2, WIDTH, HIDDEN), f32),
            pltpu.VMEM((2, HIDDEN, WIDTH), f32),
            pltpu.VMEM((CAP, WIDTH), f32),
            pltpu.SemaphoreType.DMA((15,)),
        ],
        compiler_params=pltpu.CompilerParams(vmem_limit_bytes=56 << 20),
    )(asked, returned, summed, loss)


def local(table, feature_owner, feature_offset, query_in, query_out, item_in, item_out):
    loss, asked, returned, summed = train_step(
        feature_owner.T, feature_offset.T, table, query_in, query_out, item_in, item_out
    )
    table_grad, q_in, q_out, k_in, k_out, loss = update(asked, returned, summed, loss)
    return (loss.reshape(PAIRS), table_grad, q_in, q_out, k_in, k_out)


def solution(mesh):
    in_specs = (
        P(("table", "dp"), None),
        P(("table", "dp"), None),
        P(("table", "dp"), None),
        P(),
        P(),
        P(),
        P(),
    )
    out_specs = (P(("table", "dp")), P(("table", "dp"), None), P(), P(), P(), P())
    return jax.shard_map(local, mesh=mesh, in_specs=in_specs, out_specs=out_specs, check_vma=False)
```

```python
import functools

import jax
import jax.numpy as jnp
from jax import lax
from jax.experimental import pallas as pl
from jax.experimental.pallas import tpu as pltpu
from jax.sharding import PartitionSpec as P

MESH = pl.DeviceIdType.MESH
SCALE = 20.0
SHARDS = 128
N_TABLE = 4
GROUP = 32
CAP = 16
PAIRS = 128
WIDTH = 256
HIDDEN = 1024
ROWS = 8192
QUERY_PEERS = 8
ITEM_PEERS = 4
BLOCK_Q = QUERY_PEERS * PAIRS
BLOCK_K = ITEM_PEERS * PAIRS
GRAD_ROWS = 4 * HIDDEN
HALF = GRAD_ROWS // 2
SHARE = HALF // 2
PARTS = (
    ((0, 256, (0, 1, 2)), (256, 256, (1, 2, 0)), (512, 512, (2, 0, 1))),
    ((0, 512, (0, 1, 2)), (512, 256, (1, 2, 0)), (768, 256, (2, 0, 1))),
)
N_PARTS = 6
f32 = jnp.float32
bf16 = jnp.bfloat16


def mm(a, b, contract=((1,), (0,))):
    return lax.dot_general(a, b, (contract, ((), ())), preferred_element_type=f32)


def step_kernel(
    owner_ref, offset_ref, table_ref, w_ins_ref, w_outs_ref, w_ini_ref, w_outi_ref,
    loss_ref, asked, returned_out, summed_out,
    returned, summed, table_rows, w_in, w_out, requests, asked_scalars, stage, rows, fetched, pick, pick_t,
    pre_act, hidden, unit, norm, queries, items, expo, soft, part_sums,
    q_send, q_recv, k_send, k_recv, slots, inputs, grad_out, grad_pre, core_send, core_recv, half, sum1, recv1, recv2, recv3,
    load_sems, id_recv, send_sems, recv_sems, ring_send, ring_recv, store_sems,
):
    t = lax.axis_index("table")
    dp = lax.axis_index("dp")
    me = t * GROUP + dp
    core = lax.rem(t, 2)
    z = lax.div(dp, QUERY_PEERS)
    a = lax.rem(dp, QUERY_PEERS)
    x = lax.div(a, 2)
    y = lax.rem(a, 2) * 2 + lax.div(t, 2)
    coords = (x, y, z)

    def each_ahead(u, body, first=0, last=GROUP):
        tu = lax.rem(t + u, N_TABLE)

        @pl.loop(max(first, 0 if u else 1), last, unroll=4)
        def _(v):
            body(u * GROUP + v, tu, lax.rem(dp + v, GROUP))

    def each_behind(u, body):
        tu = lax.rem(t + N_TABLE - u, N_TABLE)

        @pl.loop(0 if u else 1, GROUP)
        def _(v):
            body(u * GROUP + v, tu, lax.rem(dp + GROUP - v, GROUP))

    def chip(coords, core):
        cx, cy, cz = coords
        return (lax.rem(cy, 2) * 2 + core, cz * QUERY_PEERS + cx * 2 + lax.div(cy, 2))

    def send(src, dst, s_sem, r_sem, device):
        pltpu.make_async_remote_copy(
            src, dst, s_sem, r_sem, device_id=device, device_id_type=MESH
        ).start()

    def wait(ref, sem):
        pltpu.make_async_copy(ref, ref, sem).wait()

    loads = [
        pltpu.make_async_copy(src, dst, load_sems.at[i])
        for i, (src, dst) in enumerate(
            [
                (table_ref, table_rows),
                (w_ins_ref, w_in.at[0]),
                (w_outs_ref, w_out.at[0]),
                (w_ini_ref, w_in.at[1]),
                (w_outi_ref, w_out.at[1]),
            ]
        )
    ]
    for load in loads:
        load.start()

    barrier = pltpu.get_barrier_semaphore()

    def greet(step, tu, dv):
        pl.semaphore_signal(barrier, inc=1, device_id=(tu, dv), device_id_type=MESH)

    for u in range(N_TABLE):
        each_ahead(u, greet)

    lane = lax.broadcasted_iota(jnp.int32, (PAIRS, SHARDS), 1)
    row = lax.broadcasted_iota(jnp.int32, (PAIRS, SHARDS), 0)
    below = jnp.zeros((SHARDS - 8, PAIRS), jnp.int32)
    owner = jnp.concatenate([owner_ref[...], below], axis=0).T
    offset = jnp.concatenate([offset_ref[...], below], axis=0).T
    names = [(owner[:, k : k + 1] == lane).astype(jnp.int32) for k in range(8)]
    offsets = sum(names[k] * offset[:, k : k + 1] for k in range(8))
    named_q = sum(names[:4])
    named_k = sum(names[4:])
    named = named_q + named_k
    rank = named
    for shift in (1, 2, 4, 8, 16, 32, 64):
        rank = rank + jnp.where(row >= shift, pltpu.roll(rank, shift, 0), 0)
    rank = rank - named
    by_slot = [
        jnp.sum(jnp.where(rank == r, offsets, 0), axis=0, keepdims=True) for r in range(CAP)
    ] + [jnp.sum(named, axis=0, keepdims=True)]
    by_slot = jnp.concatenate(
        by_slot + [jnp.zeros((SHARDS - CAP - 1, SHARDS), jnp.int32)], axis=0
    )
    requests[...] = by_slot.T.reshape(SHARDS, 1, SHARDS)

    pl.semaphore_wait(barrier, SHARDS - 1)

    others = pl.ds(0, SHARDS - 1)
    asked[0] = requests[me]

    def ask(u, step, tu, dv):
        send(requests.at[tu * GROUP + dv], asked.at[step], send_sems.at[0], id_recv.at[u], (tu, dv))

    for u in range(N_TABLE):
        each_ahead(u, functools.partial(ask, u))

    def lookup(step):
        for slot in range(CAP):
            stage[slot : slot + 1, :] = table_rows[pl.ds(asked_scalars[step, 0, slot], 1), :]
        return stage[...].astype(bf16)

    def answer(step, tu, dv):
        rows[step] = lookup(step)
        send(rows.at[step], fetched.at[me], send_sems.at[1], recv_sems.at[1], (tu, dv))

    for u in range(N_TABLE):
        first = u * GROUP if u else 1
        wait(asked.at[pl.ds(first, (u + 1) * GROUP - first)], id_recv.at[u])
        at = pl.ds(u * GROUP, GROUP)
        spread = pltpu.make_async_copy(asked.at[at], asked_scalars.at[at], load_sems.at[5])
        spread.start()
        if u == 0:
            loads[0].wait()
        else:
            each_behind(u - 1, answer)
        spread.wait()
    each_behind(N_TABLE - 1, answer)
    fetched[me] = lookup(0)

    cut = 512
    rank_b, named_qb, named_kb = (v.astype(f32).astype(bf16) for v in (rank, named_q, named_k))
    for c in range(SHARDS * CAP // cut):
        col = lax.broadcasted_iota(jnp.int32, (SHARDS, cut), 1) + c * cut
        dev = lax.broadcasted_iota(jnp.int32, (SHARDS, cut), 0)
        spread_b = (lax.div(col, CAP) == dev).astype(bf16)
        hit = mm(rank_b, spread_b) == lax.rem(col, CAP).astype(f32)
        pick[0:PAIRS, c * cut : (c + 1) * cut] = jnp.where(hit, mm(named_qb, spread_b), 0.0).astype(bf16)
        pick[PAIRS:, c * cut : (c + 1) * cut] = jnp.where(hit, mm(named_kb, spread_b), 0.0).astype(bf16)
        col = lax.broadcasted_iota(jnp.int32, (cut, SHARDS), 0) + c * cut
        dev = lax.broadcasted_iota(jnp.int32, (cut, SHARDS), 1)
        spread_b = (lax.div(col, CAP) == dev).astype(bf16)
        rhs_t = ((1,), (1,))
        hit = mm(spread_b, rank_b, rhs_t) == lax.rem(col, CAP).astype(f32)
        pick_t[c * cut : (c + 1) * cut, 0:PAIRS] = jnp.where(hit, mm(spread_b, named_qb, rhs_t), 0.0).astype(bf16)
        pick_t[c * cut : (c + 1) * cut, PAIRS:] = jnp.where(hit, mm(spread_b, named_kb, rhs_t), 0.0).astype(bf16)

    for load in loads[1:]:
        load.wait()
    wait(rows.at[others], recv_sems.at[1])
    inputs[...] = (
        mm(pick[...], fetched[...].reshape(SHARDS * CAP, WIDTH)).astype(bf16).reshape(2, PAIRS, WIDTH)
    )

    for i in range(2):
        pre = mm(inputs[i], w_in[i])
        pre_act[i] = pre
        hid = (pre * lax.logistic(pre)).astype(bf16)
        hidden[i] = hid
        out = mm(hid, w_out[i])
        out_norm = jnp.sqrt(jnp.sum(out * out, axis=-1, keepdims=True) + 1e-06)
        unit[i] = out / out_norm
        norm[i] = jnp.broadcast_to(out_norm, (PAIRS, WIDTH))
        if i == 0:
            queries[a] = unit[0].astype(bf16)
            for j in range(1, QUERY_PEERS):
                peer = (t, z * QUERY_PEERS + lax.rem(a + j, QUERY_PEERS))
                send(queries.at[a], queries.at[a], send_sems.at[2], recv_sems.at[2], peer)
        else:
            items[z] = unit[1].astype(bf16)
            for j in range(1, ITEM_PEERS):
                peer = (t, lax.rem(z + j, ITEM_PEERS) * QUERY_PEERS + a)
                send(items.at[z], items.at[z], send_sems.at[3], recv_sems.at[3], peer)
    query_unit = queries[a].astype(f32)
    item_unit = items[z].astype(f32)
    wait(items.at[pl.ds(0, ITEM_PEERS - 1)], recv_sems.at[3])
    wait(queries.at[pl.ds(0, QUERY_PEERS - 1)], recv_sems.at[2])

    all_items = items[...].reshape(BLOCK_K, WIDTH)
    sums = []
    for c in range(QUERY_PEERS):
        e = jnp.exp(SCALE * mm(all_items, queries[c], ((1,), (1,))))
        expo[:, c * PAIRS : (c + 1) * PAIRS] = e
        soft[:, c * PAIRS : (c + 1) * PAIRS] = e.astype(bf16)
        sums.append(jnp.sum(e, axis=0, keepdims=True))
    part_sums[a] = jnp.concatenate(sums, axis=0)
    for j in range(1, QUERY_PEERS):
        peer = (t, z * QUERY_PEERS + lax.rem(a + j, QUERY_PEERS))
        send(part_sums.at[a], part_sums.at[a], send_sems.at[4], recv_sems.at[4], peer)

    def part_q(c):
        block = soft[:, pl.ds(pl.multiple_of(c * PAIRS, PAIRS), PAIRS)]
        return mm(block, all_items, ((0,), (0,)))

    for j in range(1, QUERY_PEERS):
        c = lax.rem(a + j, QUERY_PEERS)
        q_send[j - 1] = part_q(c).astype(bf16)
        send(q_send.at[j - 1], q_recv.at[j - 1], send_sems.at[5], recv_sems.at[5], (t, z * QUERY_PEERS + c))
    grad_q = part_q(a)
    own_score = SCALE * jnp.sum(query_unit * item_unit, axis=1, keepdims=True)
    own_score = jnp.sum(jnp.where(lane == row, own_score, 0.0), axis=0, keepdims=True)

    wait(part_sums.at[pl.ds(0, QUERY_PEERS - 1)], recv_sems.at[4])
    total = part_sums[0]
    for c in range(1, QUERY_PEERS):
        total = total + part_sums[c]
    mine = lax.broadcasted_iota(jnp.int32, (QUERY_PEERS, PAIRS), 0) == a
    own_total = jnp.sum(jnp.where(mine, total, 0.0), axis=0, keepdims=True)
    loss_ref[...] = jnp.log(own_total) - own_score
    inverse = 1.0 / total
    own_inverse = jnp.sum(jnp.where(lane == row, 1.0 / own_total, 0.0), axis=1, keepdims=True)
    for c in range(QUERY_PEERS):
        at = slice(c * PAIRS, (c + 1) * PAIRS)
        soft[:, at] = (expo[:, at] * inverse[c : c + 1, :]).astype(bf16)

    def part_k(c):
        block = soft[pl.ds(pl.multiple_of(c * PAIRS, PAIRS), PAIRS), :]
        return mm(block, queries[...].reshape(BLOCK_Q, WIDTH))

    for j in range(1, ITEM_PEERS):
        c = lax.rem(z + j, ITEM_PEERS)
        k_send[j - 1] = part_k(c).astype(bf16)
        send(k_send.at[j - 1], k_recv.at[j - 1], send_sems.at[6], recv_sems.at[6], (t, c * QUERY_PEERS + a))
    grad_k = part_k(z) - query_unit

    def back(i, grad_unit):
        u = unit[i]
        g = ((grad_unit - u * jnp.sum(grad_unit * u, axis=-1, keepdims=True)) / norm[i]).astype(bf16)
        grad_hidden = mm(g, w_out[i], ((1,), (1,)))
        pre = pre_act[i]
        s = lax.logistic(pre)
        gp = (grad_hidden * s * (1.0 + pre * (1.0 - s))).astype(bf16)
        grad_out[i] = g
        grad_pre[i] = gp

    def share_rows(i, c, block):
        at = pl.ds(pl.multiple_of((c * 2 + block % 2) * WIDTH, WIDTH), WIDTH)
        if block < 2:
            return mm(inputs[i], grad_pre[i, :, at], ((0,), (0,)))
        return mm(hidden[i, :, at], grad_out[i], ((0,), (0,)))

    def along(axis, j):
        moved = list(coords)
        moved[axis] = lax.rem(coords[axis] + j, 4)
        return moved[axis], chip(moved, core)

    def rows_at(start, size):
        return pl.ds(pl.multiple_of(start, 16), size)

    parts = ([], [])
    at1, at2 = 0, 0
    for i in range(2):
        for base, size, axes in PARTS[i]:
            parts[i].append((len(parts[0]) + len(parts[1]), i * SHARE + base, size, axes, at1, at2))
            at1, at2 = at1 + size // 4, at2 + size // 16

    def final(i, base):
        return i * HALF + core * SHARE + base - i * SHARE

    def give_core(i):
        for p, base, size, axes, at1, at2 in parts[i]:
            for r in range(base, base + size, WIDTH):
                block = (r - i * SHARE) // WIDTH
                core_send[r : r + WIDTH] = share_rows(i, 1 - core, block).astype(bf16)
            at = pl.ds(base, size)
            send(core_send.at[at], core_recv.at[at], ring_send.at[p, 0], ring_recv.at[p, 0], chip(coords, 1 - core))

    def step1(i):
        for p, base, size, axes, at1, at2 in parts[i]:
            n = size // 4
            own = [share_rows(i, core, (r - i * SHARE) // WIDTH) for r in range(base, base + size, WIDTH)]
            wait(core_recv.at[pl.ds(base, size)], ring_recv.at[p, 0])
            for k, r in enumerate(range(base, base + size, WIDTH)):
                half[r : r + WIDTH] = (own[k] + core_recv[r : r + WIDTH].astype(f32)).astype(bf16)
            for j in range(1, 4):
                c, device = along(axes[0], j)
                send(half.at[rows_at(base + c * n, n)], recv1.at[j - 1, pl.ds(at1, n)],
                     ring_send.at[p, 1], ring_recv.at[p, 1], device)

    def step2(i):
        for p, base, size, axes, at1, at2 in parts[i]:
            n, m = size // 4, size // 16
            at = pl.ds(at1, n)
            wait(recv1.at[:, at], ring_recv.at[p, 1])
            total1 = half[rows_at(base + coords[axes[0]] * n, n)].astype(f32)
            for j in range(3):
                total1 = total1 + recv1[j, at].astype(f32)
            sum1[at] = total1.astype(bf16)
            for j in range(1, 4):
                c, device = along(axes[1], j)
                send(sum1.at[rows_at(at1 + c * m, m)], recv2.at[j - 1, pl.ds(at2, m)],
                     ring_send.at[p, 2], ring_recv.at[p, 2], device)

    def step3(i):
        for p, base, size, axes, at1, at2 in parts[i]:
            m = size // 16
            at = pl.ds(at2, m)
            wait(recv2.at[:, at], ring_recv.at[p, 2])
            total2 = sum1[rows_at(at1 + coords[axes[1]] * m, m)].astype(f32)
            for j in range(3):
                total2 = total2 + recv2[j, at].astype(f32)
            c3 = coords[axes[2]]
            recv3[c3, at] = total2.astype(bf16)
            for j in range(1, 4):
                _, device = along(axes[2], j)
                send(recv3.at[c3, at], recv3.at[c3, at], ring_send.at[p, 3], ring_recv.at[p, 3], device)

    def step4(i):
        for p, base, size, axes, at1, at2 in parts[i]:
            n, m = size // 4, size // 16
            at = pl.ds(at2, m)
            wait(recv3.at[pl.ds(0, 3), at], ring_recv.at[p, 3])
            total3 = recv3[0, at].astype(f32)
            for j in range(1, 4):
                total3 = total3 + recv3[j, at].astype(f32)
            mine = rows_at(final(i, base) + coords[axes[0]] * n + coords[axes[1]] * m, m)
            summed[mine] = total3.astype(bf16)
            for j in range(1, 4):
                _, device = along(axes[1], j)
                send(summed.at[mine], summed.at[mine], ring_send.at[p, 4], ring_recv.at[p, 4], device)

    def step5(i):
        for p, base, size, axes, at1, at2 in parts[i]:
            n, m = size // 4, size // 16
            wait(summed.at[pl.ds(0, 3 * m)], ring_recv.at[p, 4])
            mine = rows_at(final(i, base) + coords[axes[0]] * n, n)
            for j in range(1, 4):
                _, device = along(axes[0], j)
                send(summed.at[mine], summed.at[mine], ring_send.at[p, 4 + j], ring_recv.at[p, 4 + j], device)
            send(summed.at[mine], summed.at[mine], ring_send.at[p, 8], ring_recv.at[p, 8], chip(coords, 1 - core))

    def step6(i):
        for j in (1, 3, 2):
            for p, base, size, axes, at1, at2 in parts[i]:
                n = size // 4
                wait(summed.at[pl.ds(0, n)], ring_recv.at[p, 4 + j])
                there = rows_at(final(i, base) + lax.rem(coords[axes[0]] + 4 - j, 4) * n, n)
                send(summed.at[there], summed.at[there], ring_send.at[p, 8], ring_recv.at[p, 8], chip(coords, 1 - core))

    def give_back(step, tu, dv):
        send(slots.at[tu * GROUP + dv], returned.at[step], send_sems.at[7], recv_sems.at[7], (tu, dv))

    wait(q_recv, recv_sems.at[5])
    for j in range(QUERY_PEERS - 1):
        grad_q = grad_q + q_recv[j].astype(f32)
    back(0, SCALE * (grad_q * own_inverse - item_unit))
    give_core(0)
    step1(0)
    wait(k_recv, recv_sems.at[6])
    for j in range(ITEM_PEERS - 1):
        grad_k = grad_k + k_recv[j].astype(f32)
    back(1, SCALE * grad_k)
    give_core(1)

    step1(1)

    grad_x = [mm(grad_pre[i], w_in[i], ((1,), (1,))).astype(bf16) for i in range(2)]
    slots[...] = (
        mm(pick_t[...], jnp.concatenate(grad_x, axis=0)).astype(bf16).reshape(SHARDS, CAP, WIDTH)
    )

    def give_run(run):
        each_ahead(run // 2, give_back, run % 2 * (GROUP // 2), (run % 2 + 1) * (GROUP // 2))

    give_run(0)
    give_run(1)
    returned[0] = slots[me]
    step2(0)
    give_run(2)
    step2(1)
    give_run(3)
    step3(0)
    give_run(4)
    step3(1)
    give_run(5)
    step4(0)
    give_run(6)
    step4(1)
    give_run(7)
    step5(0)
    step5(1)
    step6(0)
    step6(1)
    stores = []
    for p, base, size, axes, at1, at2 in parts[0] + parts[1]:
        i = base // SHARE
        wait(summed.at[pl.ds(0, size)], ring_recv.at[p, 8])
        for c in range(2):
            at = pl.ds(i * HALF + c * SHARE + base - i * SHARE, size)
            stores.append(pltpu.make_async_copy(summed.at[at], summed_out.at[at], store_sems.at[p * 2 + c]))
            stores[-1].start()

    wait(rows.at[others], recv_sems.at[7])
    stores.append(pltpu.make_async_copy(returned, returned_out, store_sems.at[2 * N_PARTS]))
    stores[-1].start()
    for ref, i in (
        (requests.at[others], 0),
        (rows.at[others], 1),
        (queries.at[pl.ds(0, QUERY_PEERS - 1)], 2),
        (items.at[pl.ds(0, ITEM_PEERS - 1)], 3),
        (part_sums.at[pl.ds(0, QUERY_PEERS - 1)], 4),
        (q_send, 5),
        (k_send, 6),
        (slots.at[others], 7),
    ):
        wait(ref, send_sems.at[i])
    for p, base, size, axes, at1, at2 in parts[0] + parts[1]:
        n, m = size // 4, size // 16
        for i, count in enumerate((size, 3 * n, 3 * m, 3 * m, 3 * m, n, n, n, size)):
            wait(summed.at[pl.ds(0, count)], ring_send.at[p, i])
    for store in stores:
        store.wait()


def train_step(owner, offset, table, query_in, query_out, item_in, item_out):
    rows1, rows2 = HALF // 4, HALF // 16
    vmem = pl.BlockSpec(memory_space=pltpu.VMEM)
    hbm = pl.BlockSpec(memory_space=pl.ANY)
    V = pltpu.VMEM
    return pl.pallas_call(
        step_kernel,
        out_shape=(
            jax.ShapeDtypeStruct((1, PAIRS), f32),
            jax.ShapeDtypeStruct((SHARDS, 1, SHARDS), jnp.int32),
            jax.ShapeDtypeStruct((SHARDS, CAP, WIDTH), bf16),
            jax.ShapeDtypeStruct((GRAD_ROWS, WIDTH), bf16),
        ),
        in_specs=[vmem, vmem, hbm, hbm, hbm, hbm, hbm],
        out_specs=(vmem, vmem, hbm, hbm),
        scratch_shapes=[
            V((SHARDS, CAP, WIDTH), bf16),
            V((GRAD_ROWS, WIDTH), bf16),
            V((ROWS, WIDTH), f32),
            V((2, WIDTH, HIDDEN), bf16),
            V((2, HIDDEN, WIDTH), bf16),
            V((SHARDS, 1, SHARDS), jnp.int32),
            pltpu.SMEM((SHARDS, 1, SHARDS), jnp.int32),
            V((CAP, WIDTH), f32),
            V((SHARDS, CAP, WIDTH), bf16),
            V((SHARDS, CAP, WIDTH), bf16),
            V((2 * PAIRS, SHARDS * CAP), bf16),
            V((SHARDS * CAP, 2 * PAIRS), bf16),
            V((2, PAIRS, HIDDEN), f32),
            V((2, PAIRS, HIDDEN), bf16),
            V((2, PAIRS, WIDTH), f32),
            V((2, PAIRS, WIDTH), f32),
            V((QUERY_PEERS, PAIRS, WIDTH), bf16),
            V((ITEM_PEERS, PAIRS, WIDTH), bf16),
            V((BLOCK_K, BLOCK_Q), f32),
            V((BLOCK_K, BLOCK_Q), bf16),
            V((QUERY_PEERS, QUERY_PEERS, PAIRS), f32),
            V((QUERY_PEERS - 1, PAIRS, WIDTH), bf16),
            V((QUERY_PEERS - 1, PAIRS, WIDTH), bf16),
            V((ITEM_PEERS - 1, PAIRS, WIDTH), bf16),
            V((ITEM_PEERS - 1, PAIRS, WIDTH), bf16),
            V((SHARDS, CAP, WIDTH), bf16),
            V((2, PAIRS, WIDTH), bf16),
            V((2, PAIRS, WIDTH), bf16),
            V((2, PAIRS, HIDDEN), bf16),
            V((HALF, WIDTH), bf16),
            V((HALF, WIDTH), bf16),
            V((HALF, WIDTH), bf16),
            V((rows1, WIDTH), bf16),
            V((3, rows1, WIDTH), bf16),
            V((3, rows2, WIDTH), bf16),
            V((4, rows2, WIDTH), bf16),
            pltpu.SemaphoreType.DMA((6,)),
            pltpu.SemaphoreType.DMA((N_TABLE,)),
            pltpu.SemaphoreType.DMA((8,)),
            pltpu.SemaphoreType.DMA((8,)),
            pltpu.SemaphoreType.DMA((N_PARTS, 9)),
            pltpu.SemaphoreType.DMA((N_PARTS, 9)),
            pltpu.SemaphoreType.DMA((2 * N_PARTS + 1,)),
        ],
        compiler_params=pltpu.CompilerParams(
            collective_id=0, has_side_effects=True, vmem_limit_bytes=56 << 20
        ),
    )(owner, offset, table, query_in, query_out, item_in, item_out)


def update_kernel(
    asked_ref, returned_ref, summed_ref, loss_ref,
    table_grad, q_in, q_out, k_in, k_out, loss_out,
    asked, returned, summed, total, other, wide_in, wide_out, stage, sems,
):
    loads = [
        pltpu.make_async_copy(src, dst, sems.at[i])
        for i, (src, dst) in enumerate(
            [(summed_ref, summed), (asked_ref, asked), (returned_ref, returned)]
        )
    ]
    for load in loads:
        load.start()
    loss_out[...] = loss_ref[...]

    @pl.loop(0, ROWS, step=256)
    def _(r):
        total[pl.ds(r, 256), :] = jnp.zeros((256, WIDTH), f32)
        other[pl.ds(r, 256), :] = jnp.zeros((256, WIDTH), f32)

    loads[0].wait()
    copies = []
    for i, (out_in, out_out) in enumerate(((q_in, q_out), (k_in, k_out))):
        base = i * HALF
        for c in range(0, HIDDEN, WIDTH):
            at = base + c // (2 * WIDTH) * SHARE + c % (2 * WIDTH)
            wide_in[i, :, c : c + WIDTH] = summed[at : at + WIDTH].astype(f32)
            at += 2 * WIDTH
            wide_out[i, c : c + WIDTH] = summed[at : at + WIDTH].astype(f32)
        copies.append(pltpu.make_async_copy(wide_in.at[i], out_in, sems.at[3 + 2 * i]))
        copies.append(pltpu.make_async_copy(wide_out.at[i], out_out, sems.at[4 + 2 * i]))
        copies[-2].start()
        copies[-1].start()
    loads[1].wait()
    loads[2].wait()

    @pl.loop(0, SHARDS, step=2)
    def _(d):
        for u in range(2):
            stage[u] = returned[d + u].astype(f32)
        count = jnp.maximum(asked[d, 0, CAP], asked[d + 1, 0, CAP])
        for first in range(0, CAP, 4):

            @pl.when(count > first)
            def _():
                for slot in range(first, first + 4, 2):
                    for u in range(2):
                        at = pl.ds(asked[d + u, 0, slot], 1)
                        at2 = pl.ds(asked[d + u, 0, slot + 1], 1)
                        total[at, :] += stage[u, slot : slot + 1, :]
                        other[at2, :] += stage[u, slot + 1 : slot + 2, :]

    cut = ROWS // 8
    for r in range(0, ROWS, cut):

        @pl.loop(r, r + cut, step=128)
        def _(q):
            total[pl.ds(q, 128), :] += other[pl.ds(q, 128), :]

        at = pl.ds(r, cut)
        copies.append(pltpu.make_async_copy(total.at[at], table_grad.at[at], sems.at[7 + r // cut]))
        copies[-1].start()
    for copy in copies:
        copy.wait()


def update(asked, returned, summed, loss):
    vmem = pl.BlockSpec(memory_space=pltpu.VMEM)
    hbm = pl.BlockSpec(memory_space=pl.ANY)
    in_shape = jax.ShapeDtypeStruct((WIDTH, HIDDEN), f32)
    out_shape = jax.ShapeDtypeStruct((HIDDEN, WIDTH), f32)
    table_shape = jax.ShapeDtypeStruct((ROWS, WIDTH), f32)
    loss_shape = jax.ShapeDtypeStruct((1, PAIRS), f32)
    return pl.pallas_call(
        update_kernel,
        out_shape=(table_shape, in_shape, out_shape, in_shape, out_shape, loss_shape),
        in_specs=[hbm, hbm, hbm, vmem],
        out_specs=(hbm,) * 5 + (vmem,),
        scratch_shapes=[
            pltpu.SMEM((SHARDS, 1, SHARDS), jnp.int32),
            pltpu.VMEM((SHARDS, CAP, WIDTH), bf16),
            pltpu.VMEM((GRAD_ROWS, WIDTH), bf16),
            pltpu.VMEM((ROWS, WIDTH), f32),
            pltpu.VMEM((ROWS, WIDTH), f32),
            pltpu.VMEM((2, WIDTH, HIDDEN), f32),
            pltpu.VMEM((2, HIDDEN, WIDTH), f32),
            pltpu.VMEM((2, CAP, WIDTH), f32),
            pltpu.SemaphoreType.DMA((15,)),
        ],
        compiler_params=pltpu.CompilerParams(vmem_limit_bytes=56 << 20),
    )(asked, returned, summed, loss)


def local(table, feature_owner, feature_offset, query_in, query_out, item_in, item_out):
    loss, asked, returned, summed = train_step(
        feature_owner.T, feature_offset.T, table, query_in, query_out, item_in, item_out
    )
    table_grad, q_in, q_out, k_in, k_out, loss = update(asked, returned, summed, loss)
    return (loss.reshape(PAIRS), table_grad, q_in, q_out, k_in, k_out)


def solution(mesh):
    in_specs = (
        P(("table", "dp"), None),
        P(("table", "dp"), None),
        P(("table", "dp"), None),
        P(),
        P(),
        P(),
        P(),
    )
    out_specs = (P(("table", "dp")), P(("table", "dp"), None), P(), P(), P(), P())
    return jax.shard_map(local, mesh=mesh, in_specs=in_specs, out_specs=out_specs, check_vma=False)
```

```python
import functools

import jax
import jax.numpy as jnp
from jax import lax
from jax.experimental import pallas as pl
from jax.experimental.pallas import tpu as pltpu
from jax.sharding import PartitionSpec as P

MESH = pl.DeviceIdType.MESH
SCALE = 20.0
SHARDS = 128
N_TABLE = 4
GROUP = 32
CAP = 16
PAIRS = 128
WIDTH = 256
HIDDEN = 1024
ROWS = 8192
QUERY_PEERS = 8
ITEM_PEERS = 4
BLOCK_Q = QUERY_PEERS * PAIRS
BLOCK_K = ITEM_PEERS * PAIRS
GRAD_ROWS = 4 * HIDDEN
HALF = GRAD_ROWS // 2
SHARE = HALF // 2
PARTS = (
    ((0, 256, (0, 1, 2)), (256, 256, (1, 2, 0)), (512, 512, (2, 0, 1))),
    ((0, 512, (0, 1, 2)), (512, 256, (1, 2, 0)), (768, 256, (2, 0, 1))),
)
N_PARTS = 6
f32 = jnp.float32
bf16 = jnp.bfloat16


def mm(a, b, contract=((1,), (0,))):
    return lax.dot_general(a, b, (contract, ((), ())), preferred_element_type=f32)


def step_kernel(
    owner_ref, offset_ref, table_ref, w_ins_ref, w_outs_ref, w_ini_ref, w_outi_ref,
    loss_ref, asked_out, returned_out, summed_out,
    asked, returned, summed, table_rows, w_in, w_out, requests, asked_scalars, stage, rows, fetched, pick, pick_t,
    pre_act, hidden, unit, norm, queries, items, expo, soft, part_sums,
    q_send, q_recv, k_send, k_recv, slots, inputs, grad_out, grad_pre, core_send, core_recv, half, sum1, recv1, recv2, recv3,
    load_sems, id_recv, row_recv, send_sems, recv_sems, ring_send, ring_recv, store_sems,
):
    t = lax.axis_index("table")
    dp = lax.axis_index("dp")
    me = t * GROUP + dp
    core = lax.rem(t, 2)
    z = lax.div(dp, QUERY_PEERS)
    a = lax.rem(dp, QUERY_PEERS)
    x = lax.div(a, 2)
    y = lax.rem(a, 2) * 2 + lax.div(t, 2)
    coords = (x, y, z)

    def each_ahead(u, body, first=0, last=GROUP):
        tu = lax.rem(t + u, N_TABLE)

        @pl.loop(max(first, 0 if u else 1), last, unroll=4)
        def _(v):
            body(u * GROUP + v, tu, lax.rem(dp + v, GROUP))

    def each_behind(u, body):
        tu = lax.rem(t + N_TABLE - u, N_TABLE)
        if u == 0:
            body(0, 1, tu, lax.rem(dp + GROUP - 1, GROUP))

        @pl.loop(0 if u else 2, GROUP, step=2)
        def _(v):
            for k in range(2):
                body(k, u * GROUP + v + k, tu, lax.rem(dp + GROUP - v - k, GROUP))

    def chip(coords, core):
        cx, cy, cz = coords
        return (lax.rem(cy, 2) * 2 + core, cz * QUERY_PEERS + cx * 2 + lax.div(cy, 2))

    def send(src, dst, s_sem, r_sem, device):
        pltpu.make_async_remote_copy(
            src, dst, s_sem, r_sem, device_id=device, device_id_type=MESH
        ).start()

    def wait(ref, sem):
        pltpu.make_async_copy(ref, ref, sem).wait()

    loads = [
        pltpu.make_async_copy(src, dst, load_sems.at[i])
        for i, (src, dst) in enumerate(
            [
                (table_ref, table_rows),
                (w_ins_ref, w_in.at[0]),
                (w_outs_ref, w_out.at[0]),
                (w_ini_ref, w_in.at[1]),
                (w_outi_ref, w_out.at[1]),
            ]
        )
    ]
    for load in loads:
        load.start()

    barrier = pltpu.get_barrier_semaphore()

    def greet(step, tu, dv):
        pl.semaphore_signal(barrier, inc=1, device_id=(tu, dv), device_id_type=MESH)

    for u in range(N_TABLE):
        each_ahead(u, greet)

    lane = lax.broadcasted_iota(jnp.int32, (PAIRS, SHARDS), 1)
    row = lax.broadcasted_iota(jnp.int32, (PAIRS, SHARDS), 0)
    below = jnp.zeros((SHARDS - 8, PAIRS), jnp.int32)
    owner = jnp.concatenate([owner_ref[...], below], axis=0).T
    offset = jnp.concatenate([offset_ref[...], below], axis=0).T
    names = [(owner[:, k : k + 1] == lane).astype(jnp.int32) for k in range(8)]
    offsets = sum(names[k] * offset[:, k : k + 1] for k in range(8))
    named_q = sum(names[:4])
    named_k = sum(names[4:])
    named = named_q + named_k
    rank = named
    for shift in (1, 2, 4, 8, 16, 32, 64):
        rank = rank + jnp.where(row >= shift, pltpu.roll(rank, shift, 0), 0)
    rank = rank - named
    by_slot = [
        jnp.sum(jnp.where(rank == r, offsets, 0), axis=0, keepdims=True) for r in range(CAP)
    ] + [jnp.sum(named, axis=0, keepdims=True)]
    by_slot = jnp.concatenate(
        by_slot + [jnp.zeros((SHARDS - CAP - 1, SHARDS), jnp.int32)], axis=0
    )
    requests[...] = by_slot.T.reshape(SHARDS, 1, SHARDS)

    pl.semaphore_wait(barrier, SHARDS - 1)

    others = pl.ds(0, SHARDS - 1)
    asked[0] = requests[me]

    def ask(u, step, tu, dv):
        send(requests.at[tu * GROUP + dv], asked.at[step], send_sems.at[0], id_recv.at[u], (tu, dv))

    for u in range(N_TABLE):
        each_ahead(u, functools.partial(ask, u))

    def lookup(k, step):
        for slot in range(CAP):
            stage[k, slot : slot + 1, :] = table_rows[pl.ds(asked_scalars[step, 0, slot], 1), :]
        return stage[k].astype(bf16)

    def answer(u, k, step, tu, dv):
        rows[step] = lookup(k, step)
        send(rows.at[step], fetched.at[me], send_sems.at[1], row_recv.at[u], (tu, dv))

    for u in range(N_TABLE):
        first = u * GROUP if u else 1
        wait(asked.at[pl.ds(first, (u + 1) * GROUP - first)], id_recv.at[u])
        at = pl.ds(u * GROUP, GROUP)
        spread = pltpu.make_async_copy(asked.at[at], asked_scalars.at[at], load_sems.at[5])
        spread.start()
        if u == 0:
            loads[0].wait()
        else:
            each_behind(u - 1, functools.partial(answer, u - 1))
        spread.wait()
    each_behind(N_TABLE - 1, functools.partial(answer, N_TABLE - 1))
    fetched[me] = lookup(0, 0)

    stores = [pltpu.make_async_copy(asked, asked_out, store_sems.at[2 * N_PARTS + 1])]
    stores[0].start()

    cut = 512
    rank_b, named_qb, named_kb = (v.astype(f32).astype(bf16) for v in (rank, named_q, named_k))
    for c in range(SHARDS * CAP // cut):
        col = lax.broadcasted_iota(jnp.int32, (SHARDS, cut), 1) + c * cut
        dev = lax.broadcasted_iota(jnp.int32, (SHARDS, cut), 0)
        spread_b = (lax.div(col, CAP) == dev).astype(bf16)
        hit = mm(rank_b, spread_b) == lax.rem(col, CAP).astype(f32)
        pick[0:PAIRS, c * cut : (c + 1) * cut] = jnp.where(hit, mm(named_qb, spread_b), 0.0).astype(bf16)
        pick[PAIRS:, c * cut : (c + 1) * cut] = jnp.where(hit, mm(named_kb, spread_b), 0.0).astype(bf16)

    for load in loads[1:]:
        load.wait()
    sums = jnp.zeros((2 * PAIRS, WIDTH), f32)
    for u in range(N_TABLE):
        count = GROUP if u else GROUP - 1
        wait(rows.at[pl.ds(0, count)], row_recv.at[u])
        tu = lax.rem(t + u, N_TABLE)
        from_group = fetched[pl.ds(tu * GROUP, GROUP)].reshape(GROUP * CAP, WIDTH)
        sums = sums + mm(pick[:, pl.ds(pl.multiple_of(tu * GROUP * CAP, GROUP * CAP), GROUP * CAP)], from_group)
    inputs[...] = sums.astype(bf16).reshape(2, PAIRS, WIDTH)

    for i in range(2):
        pre = mm(inputs[i], w_in[i])
        pre_act[i] = pre
        hid = (pre * lax.logistic(pre)).astype(bf16)
        hidden[i] = hid
        out = mm(hid, w_out[i])
        out_norm = jnp.sqrt(jnp.sum(out * out, axis=-1, keepdims=True) + 1e-06)
        unit[i] = out / out_norm
        norm[i] = jnp.broadcast_to(out_norm, (PAIRS, WIDTH))
        if i == 0:
            queries[a] = unit[0].astype(bf16)
            for j in range(1, QUERY_PEERS):
                peer = (t, z * QUERY_PEERS + lax.rem(a + j, QUERY_PEERS))
                send(queries.at[a], queries.at[a], send_sems.at[2], recv_sems.at[2], peer)
        else:
            items[z] = unit[1].astype(bf16)
            for j in range(1, ITEM_PEERS):
                peer = (t, lax.rem(z + j, ITEM_PEERS) * QUERY_PEERS + a)
                send(items.at[z], items.at[z], send_sems.at[3], recv_sems.at[3], peer)
    for c in range(SHARDS * CAP // cut):
        col = lax.broadcasted_iota(jnp.int32, (cut, SHARDS), 0) + c * cut
        dev = lax.broadcasted_iota(jnp.int32, (cut, SHARDS), 1)
        spread_b = (lax.div(col, CAP) == dev).astype(bf16)
        rhs_t = ((1,), (1,))
        hit = mm(spread_b, rank_b, rhs_t) == lax.rem(col, CAP).astype(f32)
        pick_t[c * cut : (c + 1) * cut, 0:PAIRS] = jnp.where(hit, mm(spread_b, named_qb, rhs_t), 0.0).astype(bf16)
        pick_t[c * cut : (c + 1) * cut, PAIRS:] = jnp.where(hit, mm(spread_b, named_kb, rhs_t), 0.0).astype(bf16)

    query_unit = queries[a].astype(f32)
    item_unit = items[z].astype(f32)
    wait(items.at[pl.ds(0, ITEM_PEERS - 1)], recv_sems.at[3])
    wait(queries.at[pl.ds(0, QUERY_PEERS - 1)], recv_sems.at[2])

    all_items = items[...].reshape(BLOCK_K, WIDTH)
    sums = []
    for c in range(QUERY_PEERS):
        e = jnp.exp(SCALE * mm(all_items, queries[c], ((1,), (1,))))
        expo[:, c * PAIRS : (c + 1) * PAIRS] = e
        soft[:, c * PAIRS : (c + 1) * PAIRS] = e.astype(bf16)
        sums.append(jnp.sum(e, axis=0, keepdims=True))
    part_sums[a] = jnp.concatenate(sums, axis=0)
    for j in range(1, QUERY_PEERS):
        peer = (t, z * QUERY_PEERS + lax.rem(a + j, QUERY_PEERS))
        send(part_sums.at[a], part_sums.at[a], send_sems.at[4], recv_sems.at[4], peer)

    def part_q(c):
        block = soft[:, pl.ds(pl.multiple_of(c * PAIRS, PAIRS), PAIRS)]
        return mm(block, all_items, ((0,), (0,)))

    for j in range(1, QUERY_PEERS):
        c = lax.rem(a + j, QUERY_PEERS)
        q_send[j - 1] = part_q(c).astype(bf16)
        send(q_send.at[j - 1], q_recv.at[j - 1], send_sems.at[5], recv_sems.at[5], (t, z * QUERY_PEERS + c))
    grad_q = part_q(a)
    own_score = SCALE * jnp.sum(query_unit * item_unit, axis=1, keepdims=True)
    own_score = jnp.sum(jnp.where(lane == row, own_score, 0.0), axis=0, keepdims=True)

    wait(part_sums.at[pl.ds(0, QUERY_PEERS - 1)], recv_sems.at[4])
    total = part_sums[0]
    for c in range(1, QUERY_PEERS):
        total = total + part_sums[c]
    mine = lax.broadcasted_iota(jnp.int32, (QUERY_PEERS, PAIRS), 0) == a
    own_total = jnp.sum(jnp.where(mine, total, 0.0), axis=0, keepdims=True)
    loss_ref[...] = jnp.log(own_total) - own_score
    inverse = 1.0 / total
    own_inverse = jnp.sum(jnp.where(lane == row, 1.0 / own_total, 0.0), axis=1, keepdims=True)
    for c in range(QUERY_PEERS):
        at = slice(c * PAIRS, (c + 1) * PAIRS)
        soft[:, at] = (expo[:, at] * inverse[c : c + 1, :]).astype(bf16)

    def part_k(c):
        block = soft[pl.ds(pl.multiple_of(c * PAIRS, PAIRS), PAIRS), :]
        return mm(block, queries[...].reshape(BLOCK_Q, WIDTH))

    for j in range(1, ITEM_PEERS):
        c = lax.rem(z + j, ITEM_PEERS)
        k_send[j - 1] = part_k(c).astype(bf16)
        send(k_send.at[j - 1], k_recv.at[j - 1], send_sems.at[6], recv_sems.at[6], (t, c * QUERY_PEERS + a))
    grad_k = part_k(z) - query_unit

    def back(i, grad_unit):
        u = unit[i]
        g = ((grad_unit - u * jnp.sum(grad_unit * u, axis=-1, keepdims=True)) / norm[i]).astype(bf16)
        grad_hidden = mm(g, w_out[i], ((1,), (1,)))
        pre = pre_act[i]
        s = lax.logistic(pre)
        gp = (grad_hidden * s * (1.0 + pre * (1.0 - s))).astype(bf16)
        grad_out[i] = g
        grad_pre[i] = gp

    def share_rows(i, c, block):
        at = pl.ds(pl.multiple_of((c * 2 + block % 2) * WIDTH, WIDTH), WIDTH)
        if block < 2:
            return mm(inputs[i], grad_pre[i, :, at], ((0,), (0,)))
        return mm(hidden[i, :, at], grad_out[i], ((0,), (0,)))

    def along(axis, j):
        moved = list(coords)
        moved[axis] = lax.rem(coords[axis] + j, 4)
        return moved[axis], chip(moved, core)

    def rows_at(start, size):
        return pl.ds(pl.multiple_of(start, 16), size)

    parts = ([], [])
    at1, at2 = 0, 0
    for i in range(2):
        for base, size, axes in PARTS[i]:
            parts[i].append((len(parts[0]) + len(parts[1]), i * SHARE + base, size, axes, at1, at2))
            at1, at2 = at1 + size // 4, at2 + size // 16

    def final(i, base):
        return i * HALF + core * SHARE + base - i * SHARE

    def give_core(i):
        for p, base, size, axes, at1, at2 in parts[i]:
            for r in range(base, base + size, WIDTH):
                block = (r - i * SHARE) // WIDTH
                core_send[r : r + WIDTH] = share_rows(i, 1 - core, block).astype(bf16)
            at = pl.ds(base, size)
            send(core_send.at[at], core_recv.at[at], ring_send.at[p, 0], ring_recv.at[p, 0], chip(coords, 1 - core))

    def step1(i):
        for p, base, size, axes, at1, at2 in parts[i]:
            n = size // 4
            own = [share_rows(i, core, (r - i * SHARE) // WIDTH) for r in range(base, base + size, WIDTH)]
            wait(core_recv.at[pl.ds(base, size)], ring_recv.at[p, 0])
            for k, r in enumerate(range(base, base + size, WIDTH)):
                half[r : r + WIDTH] = (own[k] + core_recv[r : r + WIDTH].astype(f32)).astype(bf16)
            for j in range(1, 4):
                c, device = along(axes[0], j)
                send(half.at[rows_at(base + c * n, n)], recv1.at[j - 1, pl.ds(at1, n)],
                     ring_send.at[p, 1], ring_recv.at[p, 1], device)

    def step2(i):
        for p, base, size, axes, at1, at2 in parts[i]:
            n, m = size // 4, size // 16
            at = pl.ds(at1, n)
            wait(recv1.at[:, at], ring_recv.at[p, 1])
            total1 = half[rows_at(base + coords[axes[0]] * n, n)].astype(f32)
            for j in range(3):
                total1 = total1 + recv1[j, at].astype(f32)
            sum1[at] = total1.astype(bf16)
            for j in range(1, 4):
                c, device = along(axes[1], j)
                send(sum1.at[rows_at(at1 + c * m, m)], recv2.at[j - 1, pl.ds(at2, m)],
                     ring_send.at[p, 2], ring_recv.at[p, 2], device)

    def step3(i):
        for p, base, size, axes, at1, at2 in parts[i]:
            m = size // 16
            at = pl.ds(at2, m)
            wait(recv2.at[:, at], ring_recv.at[p, 2])
            total2 = sum1[rows_at(at1 + coords[axes[1]] * m, m)].astype(f32)
            for j in range(3):
                total2 = total2 + recv2[j, at].astype(f32)
            c3 = coords[axes[2]]
            recv3[c3, at] = total2.astype(bf16)
            for j in range(1, 4):
                _, device = along(axes[2], j)
                send(recv3.at[c3, at], recv3.at[c3, at], ring_send.at[p, 3], ring_recv.at[p, 3], device)

    def step4(i):
        for p, base, size, axes, at1, at2 in parts[i]:
            n, m = size // 4, size // 16
            at = pl.ds(at2, m)
            wait(recv3.at[pl.ds(0, 3), at], ring_recv.at[p, 3])
            total3 = recv3[0, at].astype(f32)
            for j in range(1, 4):
                total3 = total3 + recv3[j, at].astype(f32)
            mine = rows_at(final(i, base) + coords[axes[0]] * n + coords[axes[1]] * m, m)
            summed[mine] = total3.astype(bf16)
            for j in range(1, 4):
                _, device = along(axes[1], j)
                send(summed.at[mine], summed.at[mine], ring_send.at[p, 4], ring_recv.at[p, 4], device)

    def step5(i):
        for p, base, size, axes, at1, at2 in parts[i]:
            n, m = size // 4, size // 16
            wait(summed.at[pl.ds(0, 3 * m)], ring_recv.at[p, 4])
            mine = rows_at(final(i, base) + coords[axes[0]] * n, n)
            for j in range(1, 4):
                _, device = along(axes[0], j)
                send(summed.at[mine], summed.at[mine], ring_send.at[p, 4 + j], ring_recv.at[p, 4 + j], device)
            send(summed.at[mine], summed.at[mine], ring_send.at[p, 8], ring_recv.at[p, 8], chip(coords, 1 - core))

    def step6(i):
        for j in (1, 3, 2):
            for p, base, size, axes, at1, at2 in parts[i]:
                n = size // 4
                wait(summed.at[pl.ds(0, n)], ring_recv.at[p, 4 + j])
                there = rows_at(final(i, base) + lax.rem(coords[axes[0]] + 4 - j, 4) * n, n)
                send(summed.at[there], summed.at[there], ring_send.at[p, 8], ring_recv.at[p, 8], chip(coords, 1 - core))

    def give_back(step, tu, dv):
        send(slots.at[tu * GROUP + dv], returned.at[step], send_sems.at[7], recv_sems.at[7], (tu, dv))

    wait(q_recv, recv_sems.at[5])
    for j in range(QUERY_PEERS - 1):
        grad_q = grad_q + q_recv[j].astype(f32)
    back(0, SCALE * (grad_q * own_inverse - item_unit))
    give_core(0)
    step1(0)
    wait(k_recv, recv_sems.at[6])
    for j in range(ITEM_PEERS - 1):
        grad_k = grad_k + k_recv[j].astype(f32)
    back(1, SCALE * grad_k)
    give_core(1)

    step1(1)

    grad_x = [mm(grad_pre[i], w_in[i], ((1,), (1,))).astype(bf16) for i in range(2)]
    slots[...] = (
        mm(pick_t[...], jnp.concatenate(grad_x, axis=0)).astype(bf16).reshape(SHARDS, CAP, WIDTH)
    )

    def wait_sent(first, last):
        for p, base, size, axes, at1, at2 in parts[0] + parts[1]:
            n, m = size // 4, size // 16
            counts = (size, 3 * n, 3 * m, 3 * m, 3 * m, n, n, n, size)
            for i in range(first, last):
                wait(summed.at[pl.ds(0, counts[i])], ring_send.at[p, i])

    def give_run(run):
        each_ahead(run // 2, give_back, run % 2 * (GROUP // 2), (run % 2 + 1) * (GROUP // 2))

    give_run(0)
    give_run(1)
    returned[0] = slots[me]
    step2(0)
    give_run(2)
    for ref, i in (
        (requests.at[others], 0),
        (rows.at[others], 1),
        (queries.at[pl.ds(0, QUERY_PEERS - 1)], 2),
        (items.at[pl.ds(0, ITEM_PEERS - 1)], 3),
        (part_sums.at[pl.ds(0, QUERY_PEERS - 1)], 4),
        (q_send, 5),
        (k_send, 6),
    ):
        wait(ref, send_sems.at[i])
    step2(1)
    give_run(3)
    step3(0)
    give_run(4)
    step3(1)
    give_run(5)
    step4(0)
    give_run(6)
    step4(1)
    give_run(7)
    step5(0)
    step5(1)
    wait_sent(0, 4)
    step6(0)
    step6(1)
    for p, base, size, axes, at1, at2 in parts[0] + parts[1]:
        i = base // SHARE
        wait(summed.at[pl.ds(0, size)], ring_recv.at[p, 8])
        for c in range(2):
            at = pl.ds(i * HALF + c * SHARE + base - i * SHARE, size)
            stores.append(pltpu.make_async_copy(summed.at[at], summed_out.at[at], store_sems.at[p * 2 + c]))
            stores[-1].start()

    wait(rows.at[others], recv_sems.at[7])
    stores.append(pltpu.make_async_copy(returned, returned_out, store_sems.at[2 * N_PARTS]))
    stores[-1].start()
    wait(slots.at[others], send_sems.at[7])
    wait_sent(4, 9)
    for store in stores:
        store.wait()


def train_step(owner, offset, table, query_in, query_out, item_in, item_out):
    rows1, rows2 = HALF // 4, HALF // 16
    vmem = pl.BlockSpec(memory_space=pltpu.VMEM)
    hbm = pl.BlockSpec(memory_space=pl.ANY)
    V = pltpu.VMEM
    return pl.pallas_call(
        step_kernel,
        out_shape=(
            jax.ShapeDtypeStruct((1, PAIRS), f32),
            jax.ShapeDtypeStruct((SHARDS, 1, SHARDS), jnp.int32),
            jax.ShapeDtypeStruct((SHARDS, CAP, WIDTH), bf16),
            jax.ShapeDtypeStruct((GRAD_ROWS, WIDTH), bf16),
        ),
        in_specs=[vmem, vmem, hbm, hbm, hbm, hbm, hbm],
        out_specs=(vmem, hbm, hbm, hbm),
        scratch_shapes=[
            V((SHARDS, 1, SHARDS), jnp.int32),
            V((SHARDS, CAP, WIDTH), bf16),
            V((GRAD_ROWS, WIDTH), bf16),
            V((ROWS, WIDTH), f32),
            V((2, WIDTH, HIDDEN), bf16),
            V((2, HIDDEN, WIDTH), bf16),
            V((SHARDS, 1, SHARDS), jnp.int32),
            pltpu.SMEM((SHARDS, 1, SHARDS), jnp.int32),
            V((2, CAP, WIDTH), f32),
            V((SHARDS, CAP, WIDTH), bf16),
            V((SHARDS, CAP, WIDTH), bf16),
            V((2 * PAIRS, SHARDS * CAP), bf16),
            V((SHARDS * CAP, 2 * PAIRS), bf16),
            V((2, PAIRS, HIDDEN), f32),
            V((2, PAIRS, HIDDEN), bf16),
            V((2, PAIRS, WIDTH), f32),
            V((2, PAIRS, WIDTH), f32),
            V((QUERY_PEERS, PAIRS, WIDTH), bf16),
            V((ITEM_PEERS, PAIRS, WIDTH), bf16),
            V((BLOCK_K, BLOCK_Q), f32),
            V((BLOCK_K, BLOCK_Q), bf16),
            V((QUERY_PEERS, QUERY_PEERS, PAIRS), f32),
            V((QUERY_PEERS - 1, PAIRS, WIDTH), bf16),
            V((QUERY_PEERS - 1, PAIRS, WIDTH), bf16),
            V((ITEM_PEERS - 1, PAIRS, WIDTH), bf16),
            V((ITEM_PEERS - 1, PAIRS, WIDTH), bf16),
            V((SHARDS, CAP, WIDTH), bf16),
            V((2, PAIRS, WIDTH), bf16),
            V((2, PAIRS, WIDTH), bf16),
            V((2, PAIRS, HIDDEN), bf16),
            V((HALF, WIDTH), bf16),
            V((HALF, WIDTH), bf16),
            V((HALF, WIDTH), bf16),
            V((rows1, WIDTH), bf16),
            V((3, rows1, WIDTH), bf16),
            V((3, rows2, WIDTH), bf16),
            V((4, rows2, WIDTH), bf16),
            pltpu.SemaphoreType.DMA((6,)),
            pltpu.SemaphoreType.DMA((N_TABLE,)),
            pltpu.SemaphoreType.DMA((N_TABLE,)),
            pltpu.SemaphoreType.DMA((8,)),
            pltpu.SemaphoreType.DMA((8,)),
            pltpu.SemaphoreType.DMA((N_PARTS, 9)),
            pltpu.SemaphoreType.DMA((N_PARTS, 9)),
            pltpu.SemaphoreType.DMA((2 * N_PARTS + 2,)),
        ],
        compiler_params=pltpu.CompilerParams(
            collective_id=0, has_side_effects=True, vmem_limit_bytes=56 << 20
        ),
    )(owner, offset, table, query_in, query_out, item_in, item_out)


def update_kernel(
    asked_ref, returned_ref, summed_ref, loss_ref,
    table_grad, q_in, q_out, k_in, k_out, loss_out,
    asked, returned, summed, total, other, wide_in, wide_out, stage, sems,
):
    loads = [
        pltpu.make_async_copy(src, dst, sems.at[i])
        for i, (src, dst) in enumerate(
            [(summed_ref, summed), (asked_ref, asked), (returned_ref, returned)]
        )
    ]
    for load in loads:
        load.start()
    loss_out[...] = loss_ref[...]

    @pl.loop(0, ROWS, step=256)
    def _(r):
        total[pl.ds(r, 256), :] = jnp.zeros((256, WIDTH), f32)
        other[pl.ds(r, 256), :] = jnp.zeros((256, WIDTH), f32)

    loads[0].wait()
    copies = []
    for i, (out_in, out_out) in enumerate(((q_in, q_out), (k_in, k_out))):
        base = i * HALF
        for c in range(0, HIDDEN, WIDTH):
            at = base + c // (2 * WIDTH) * SHARE + c % (2 * WIDTH)
            wide_in[i, :, c : c + WIDTH] = summed[at : at + WIDTH].astype(f32)
            at += 2 * WIDTH
            wide_out[i, c : c + WIDTH] = summed[at : at + WIDTH].astype(f32)
        copies.append(pltpu.make_async_copy(wide_in.at[i], out_in, sems.at[3 + 2 * i]))
        copies.append(pltpu.make_async_copy(wide_out.at[i], out_out, sems.at[4 + 2 * i]))
        copies[-2].start()
        copies[-1].start()
    loads[1].wait()
    loads[2].wait()

    @pl.loop(0, SHARDS, step=2)
    def _(d):
        for u in range(2):
            stage[u] = returned[d + u].astype(f32)
        count = jnp.maximum(asked[d, 0, CAP], asked[d + 1, 0, CAP])
        for first in range(0, CAP, 4):

            @pl.when(count > first)
            def _():
                for slot in range(first, first + 4, 2):
                    for u in range(2):
                        at = pl.ds(asked[d + u, 0, slot], 1)
                        at2 = pl.ds(asked[d + u, 0, slot + 1], 1)
                        total[at, :] += stage[u, slot : slot + 1, :]
                        other[at2, :] += stage[u, slot + 1 : slot + 2, :]

    cut = ROWS // 8
    for r in range(0, ROWS, cut):

        @pl.loop(r, r + cut, step=128)
        def _(q):
            total[pl.ds(q, 128), :] += other[pl.ds(q, 128), :]

        at = pl.ds(r, cut)
        copies.append(pltpu.make_async_copy(total.at[at], table_grad.at[at], sems.at[7 + r // cut]))
        copies[-1].start()
    for copy in copies:
        copy.wait()


def update(asked, returned, summed, loss):
    vmem = pl.BlockSpec(memory_space=pltpu.VMEM)
    hbm = pl.BlockSpec(memory_space=pl.ANY)
    in_shape = jax.ShapeDtypeStruct((WIDTH, HIDDEN), f32)
    out_shape = jax.ShapeDtypeStruct((HIDDEN, WIDTH), f32)
    table_shape = jax.ShapeDtypeStruct((ROWS, WIDTH), f32)
    loss_shape = jax.ShapeDtypeStruct((1, PAIRS), f32)
    return pl.pallas_call(
        update_kernel,
        out_shape=(table_shape, in_shape, out_shape, in_shape, out_shape, loss_shape),
        in_specs=[hbm, hbm, hbm, vmem],
        out_specs=(hbm,) * 5 + (vmem,),
        scratch_shapes=[
            pltpu.SMEM((SHARDS, 1, SHARDS), jnp.int32),
            pltpu.VMEM((SHARDS, CAP, WIDTH), bf16),
            pltpu.VMEM((GRAD_ROWS, WIDTH), bf16),
            pltpu.VMEM((ROWS, WIDTH), f32),
            pltpu.VMEM((ROWS, WIDTH), f32),
            pltpu.VMEM((2, WIDTH, HIDDEN), f32),
            pltpu.VMEM((2, HIDDEN, WIDTH), f32),
            pltpu.VMEM((2, CAP, WIDTH), f32),
            pltpu.SemaphoreType.DMA((15,)),
        ],
        compiler_params=pltpu.CompilerParams(vmem_limit_bytes=56 << 20),
    )(asked, returned, summed, loss)


def local(table, feature_owner, feature_offset, query_in, query_out, item_in, item_out):
    loss, asked, returned, summed = train_step(
        feature_owner.T, feature_offset.T, table, query_in, query_out, item_in, item_out
    )
    table_grad, q_in, q_out, k_in, k_out, loss = update(asked, returned, summed, loss)
    return (loss.reshape(PAIRS), table_grad, q_in, q_out, k_in, k_out)


def solution(mesh):
    in_specs = (
        P(("table", "dp"), None),
        P(("table", "dp"), None),
        P(("table", "dp"), None),
        P(),
        P(),
        P(),
        P(),
    )
    out_specs = (P(("table", "dp")), P(("table", "dp"), None), P(), P(), P(), P())
    return jax.shard_map(local, mesh=mesh, in_specs=in_specs, out_specs=out_specs, check_vma=False)
```

```python
import functools

import jax
import jax.numpy as jnp
from jax import lax
from jax.experimental import pallas as pl
from jax.experimental.pallas import tpu as pltpu
from jax.sharding import PartitionSpec as P

MESH = pl.DeviceIdType.MESH
SCALE = 20.0
SHARDS = 128
N_TABLE = 4
GROUP = 32
CAP = 16
PAIRS = 128
WIDTH = 256
HIDDEN = 1024
ROWS = 8192
QUERY_PEERS = 8
ITEM_PEERS = 4
BLOCK_Q = QUERY_PEERS * PAIRS
BLOCK_K = ITEM_PEERS * PAIRS
GRAD_ROWS = 4 * HIDDEN
HALF = GRAD_ROWS // 2
SHARE = HALF // 2
PARTS = (
    ((0, 256, (0, 1, 2)), (256, 256, (1, 2, 0)), (512, 512, (2, 0, 1))),
    ((0, 512, (0, 1, 2)), (512, 256, (1, 2, 0)), (768, 256, (2, 0, 1))),
)
N_PARTS = 6
f32 = jnp.float32
bf16 = jnp.bfloat16


def mm(a, b, contract=((1,), (0,))):
    return lax.dot_general(a, b, (contract, ((), ())), preferred_element_type=f32)


def step_kernel(
    owner_ref, offset_ref, table_ref, w_ins_ref, w_outs_ref, w_ini_ref, w_outi_ref,
    loss_ref, asked_out, returned_out, summed_out,
    asked, returned, summed, table_rows, w_in, w_out, requests, asked_scalars, stage, rows, fetched, pick, pick_t,
    pre_act, hidden, unit, norm, queries, items, expo, soft, part_sums,
    q_send, q_recv, k_send, k_recv, slots, inputs, grad_out, grad_pre, core_send, core_recv, half, sum1, recv1, recv2, recv3,
    load_sems, id_recv, row_recv, send_sems, recv_sems, ring_send, ring_recv, store_sems,
):
    t = lax.axis_index("table")
    dp = lax.axis_index("dp")
    me = t * GROUP + dp
    core = lax.rem(t, 2)
    z = lax.div(dp, QUERY_PEERS)
    a = lax.rem(dp, QUERY_PEERS)
    x = lax.div(a, 2)
    y = lax.rem(a, 2) * 2 + lax.div(t, 2)
    coords = (x, y, z)

    def each_ahead(u, body, first=0, last=GROUP):
        tu = lax.rem(t + u, N_TABLE)

        @pl.loop(max(first, 0 if u else 1), last, unroll=4)
        def _(v):
            body(u * GROUP + v, tu, lax.rem(dp + v, GROUP))

    def each_behind(u, body):
        tu = lax.rem(t + N_TABLE - u, N_TABLE)
        if u == 0:
            body(0, 1, tu, lax.rem(dp + GROUP - 1, GROUP))

        @pl.loop(0 if u else 2, GROUP, step=2)
        def _(v):
            for k in range(2):
                body(k, u * GROUP + v + k, tu, lax.rem(dp + GROUP - v - k, GROUP))

    def chip(coords, core):
        cx, cy, cz = coords
        return (lax.rem(cy, 2) * 2 + core, cz * QUERY_PEERS + cx * 2 + lax.div(cy, 2))

    def send(src, dst, s_sem, r_sem, device):
        pltpu.make_async_remote_copy(
            src, dst, s_sem, r_sem, device_id=device, device_id_type=MESH
        ).start()

    def wait(ref, sem):
        pltpu.make_async_copy(ref, ref, sem).wait()

    loads = [
        pltpu.make_async_copy(src, dst, load_sems.at[i])
        for i, (src, dst) in enumerate(
            [
                (table_ref, table_rows),
                (w_ins_ref, w_in.at[0]),
                (w_outs_ref, w_out.at[0]),
                (w_ini_ref, w_in.at[1]),
                (w_outi_ref, w_out.at[1]),
            ]
        )
    ]
    for load in loads:
        load.start()

    barrier = pltpu.get_barrier_semaphore()

    def greet(step, tu, dv):
        pl.semaphore_signal(barrier, inc=1, device_id=(tu, dv), device_id_type=MESH)

    for u in range(N_TABLE):
        each_ahead(u, greet)

    lane = lax.broadcasted_iota(jnp.int32, (PAIRS, SHARDS), 1)
    row = lax.broadcasted_iota(jnp.int32, (PAIRS, SHARDS), 0)
    below = jnp.zeros((SHARDS - 8, PAIRS), jnp.int32)
    owner = jnp.concatenate([owner_ref[...], below], axis=0).T
    offset = jnp.concatenate([offset_ref[...], below], axis=0).T
    names = [(owner[:, k : k + 1] == lane).astype(jnp.int32) for k in range(8)]
    offsets = sum(names[k] * offset[:, k : k + 1] for k in range(8))
    named_q = sum(names[:4])
    named_k = sum(names[4:])
    named = named_q + named_k
    rank = named
    for shift in (1, 2, 4, 8, 16, 32, 64):
        rank = rank + jnp.where(row >= shift, pltpu.roll(rank, shift, 0), 0)
    rank = rank - named
    by_slot = [
        jnp.sum(jnp.where(rank == r, offsets, 0), axis=0, keepdims=True) for r in range(CAP)
    ] + [jnp.sum(named, axis=0, keepdims=True)]
    by_slot = jnp.concatenate(
        by_slot + [jnp.zeros((SHARDS - CAP - 1, SHARDS), jnp.int32)], axis=0
    )
    requests[...] = by_slot.T.reshape(SHARDS, 1, SHARDS)

    pl.semaphore_wait(barrier, SHARDS - 1)

    others = pl.ds(0, SHARDS - 1)
    asked[0] = requests[me]

    def ask(u, step, tu, dv):
        send(requests.at[tu * GROUP + dv], asked.at[step], send_sems.at[0], id_recv.at[u], (tu, dv))

    for u in range(N_TABLE):
        each_ahead(u, functools.partial(ask, u))

    def lookup(k, step):
        for slot in range(CAP):
            stage[k, slot : slot + 1, :] = table_rows[pl.ds(asked_scalars[step, 0, slot], 1), :]
        return stage[k].astype(bf16)

    def answer(u, k, step, tu, dv):
        rows[step] = lookup(k, step)
        send(rows.at[step], fetched.at[me], send_sems.at[1], row_recv.at[u], (tu, dv))

    for u in range(N_TABLE):
        first = u * GROUP if u else 1
        wait(asked.at[pl.ds(first, (u + 1) * GROUP - first)], id_recv.at[u])
        at = pl.ds(u * GROUP, GROUP)
        spread = pltpu.make_async_copy(asked.at[at], asked_scalars.at[at], load_sems.at[5])
        spread.start()
        if u == 0:
            loads[0].wait()
        else:
            each_behind(u - 1, functools.partial(answer, u - 1))
        spread.wait()
    each_behind(N_TABLE - 1, functools.partial(answer, N_TABLE - 1))
    fetched[me] = lookup(0, 0)

    stores = [pltpu.make_async_copy(asked, asked_out, store_sems.at[2 * N_PARTS + 1])]
    stores[0].start()

    cut = 512
    rank_b, named_qb, named_kb = (v.astype(f32).astype(bf16) for v in (rank, named_q, named_k))
    for c in range(SHARDS * CAP // cut):
        col = lax.broadcasted_iota(jnp.int32, (SHARDS, cut), 1) + c * cut
        dev = lax.broadcasted_iota(jnp.int32, (SHARDS, cut), 0)
        spread_b = (lax.div(col, CAP) == dev).astype(bf16)
        hit = mm(rank_b, spread_b) == lax.rem(col, CAP).astype(f32)
        pick[0:PAIRS, c * cut : (c + 1) * cut] = jnp.where(hit, mm(named_qb, spread_b), 0.0).astype(bf16)
        pick[PAIRS:, c * cut : (c + 1) * cut] = jnp.where(hit, mm(named_kb, spread_b), 0.0).astype(bf16)

    for load in loads[1:]:
        load.wait()
    sums = jnp.zeros((2 * PAIRS, WIDTH), f32)
    for u in range(N_TABLE):
        count = GROUP if u else GROUP - 1
        wait(rows.at[pl.ds(0, count)], row_recv.at[u])
        tu = lax.rem(t + u, N_TABLE)
        from_group = fetched[pl.ds(tu * GROUP, GROUP)].reshape(GROUP * CAP, WIDTH)
        sums = sums + mm(pick[:, pl.ds(pl.multiple_of(tu * GROUP * CAP, GROUP * CAP), GROUP * CAP)], from_group)
    inputs[...] = sums.astype(bf16).reshape(2, PAIRS, WIDTH)

    for i in range(2):
        pre = mm(inputs[i], w_in[i])
        pre_act[i] = pre
        hid = (pre * lax.logistic(pre)).astype(bf16)
        hidden[i] = hid
        out = mm(hid, w_out[i])
        out_norm = jnp.sqrt(jnp.sum(out * out, axis=-1, keepdims=True) + 1e-06)
        unit[i] = out / out_norm
        norm[i] = jnp.broadcast_to(out_norm, (PAIRS, WIDTH))
        if i == 0:
            queries[a] = unit[0].astype(bf16)
            for j in range(1, QUERY_PEERS):
                peer = (t, z * QUERY_PEERS + lax.rem(a + j, QUERY_PEERS))
                send(queries.at[a], queries.at[a], send_sems.at[2], recv_sems.at[2], peer)
        else:
            items[z] = unit[1].astype(bf16)
            for j in range(1, ITEM_PEERS):
                peer = (t, lax.rem(z + j, ITEM_PEERS) * QUERY_PEERS + a)
                send(items.at[z], items.at[z], send_sems.at[3], recv_sems.at[3], peer)
    for c in range(SHARDS * CAP // cut):
        col = lax.broadcasted_iota(jnp.int32, (cut, SHARDS), 0) + c * cut
        dev = lax.broadcasted_iota(jnp.int32, (cut, SHARDS), 1)
        spread_b = (lax.div(col, CAP) == dev).astype(bf16)
        rhs_t = ((1,), (1,))
        hit = mm(spread_b, rank_b, rhs_t) == lax.rem(col, CAP).astype(f32)
        pick_t[c * cut : (c + 1) * cut, 0:PAIRS] = jnp.where(hit, mm(spread_b, named_qb, rhs_t), 0.0).astype(bf16)
        pick_t[c * cut : (c + 1) * cut, PAIRS:] = jnp.where(hit, mm(spread_b, named_kb, rhs_t), 0.0).astype(bf16)

    query_unit = queries[a].astype(f32)
    item_unit = items[z].astype(f32)
    wait(items.at[pl.ds(0, ITEM_PEERS - 1)], recv_sems.at[3])
    wait(queries.at[pl.ds(0, QUERY_PEERS - 1)], recv_sems.at[2])

    all_items = items[...].reshape(BLOCK_K, WIDTH)
    sums = []
    for c in range(QUERY_PEERS):
        e = jnp.exp(SCALE * mm(all_items, queries[c], ((1,), (1,))))
        expo[:, c * PAIRS : (c + 1) * PAIRS] = e
        soft[:, c * PAIRS : (c + 1) * PAIRS] = e.astype(bf16)
        sums.append(jnp.sum(e, axis=0, keepdims=True))
    part_sums[a] = jnp.concatenate(sums, axis=0)
    for j in range(1, QUERY_PEERS):
        peer = (t, z * QUERY_PEERS + lax.rem(a + j, QUERY_PEERS))
        send(part_sums.at[a], part_sums.at[a], send_sems.at[4], recv_sems.at[4], peer)

    def part_q(c):
        block = soft[:, pl.ds(pl.multiple_of(c * PAIRS, PAIRS), PAIRS)]
        return mm(block, all_items, ((0,), (0,)))

    for j in range(1, QUERY_PEERS):
        c = lax.rem(a + j, QUERY_PEERS)
        q_send[j - 1] = part_q(c).astype(bf16)
        send(q_send.at[j - 1], q_recv.at[j - 1], send_sems.at[5], recv_sems.at[5], (t, z * QUERY_PEERS + c))
    grad_q = part_q(a)
    own_score = SCALE * jnp.sum(query_unit * item_unit, axis=1, keepdims=True)
    own_score = jnp.sum(jnp.where(lane == row, own_score, 0.0), axis=0, keepdims=True)

    wait(part_sums.at[pl.ds(0, QUERY_PEERS - 1)], recv_sems.at[4])
    total = part_sums[0]
    for c in range(1, QUERY_PEERS):
        total = total + part_sums[c]
    mine = lax.broadcasted_iota(jnp.int32, (QUERY_PEERS, PAIRS), 0) == a
    own_total = jnp.sum(jnp.where(mine, total, 0.0), axis=0, keepdims=True)
    loss_ref[...] = jnp.log(own_total) - own_score
    inverse = 1.0 / total
    own_inverse = jnp.sum(jnp.where(lane == row, 1.0 / own_total, 0.0), axis=1, keepdims=True)
    for c in range(QUERY_PEERS):
        at = slice(c * PAIRS, (c + 1) * PAIRS)
        soft[:, at] = (expo[:, at] * inverse[c : c + 1, :]).astype(bf16)

    def part_k(c):
        block = soft[pl.ds(pl.multiple_of(c * PAIRS, PAIRS), PAIRS), :]
        return mm(block, queries[...].reshape(BLOCK_Q, WIDTH))

    for j in range(1, ITEM_PEERS):
        c = lax.rem(z + j, ITEM_PEERS)
        k_send[j - 1] = part_k(c).astype(bf16)
        send(k_send.at[j - 1], k_recv.at[j - 1], send_sems.at[6], recv_sems.at[6], (t, c * QUERY_PEERS + a))
    grad_k = part_k(z) - query_unit

    def back(i, grad_unit):
        u = unit[i]
        g = ((grad_unit - u * jnp.sum(grad_unit * u, axis=-1, keepdims=True)) / norm[i]).astype(bf16)
        grad_hidden = mm(g, w_out[i], ((1,), (1,)))
        pre = pre_act[i]
        s = lax.logistic(pre)
        gp = (grad_hidden * s * (1.0 + pre * (1.0 - s))).astype(bf16)
        grad_out[i] = g
        grad_pre[i] = gp

    def share_rows(i, c, block):
        at = pl.ds(pl.multiple_of((c * 2 + block % 2) * WIDTH, WIDTH), WIDTH)
        if block < 2:
            return mm(inputs[i], grad_pre[i, :, at], ((0,), (0,)))
        return mm(hidden[i, :, at], grad_out[i], ((0,), (0,)))

    def along(axis, j):
        moved = list(coords)
        moved[axis] = lax.rem(coords[axis] + j, 4)
        return moved[axis], chip(moved, core)

    def rows_at(start, size):
        return pl.ds(pl.multiple_of(start, 16), size)

    parts = ([], [])
    at1, at2 = 0, 0
    for i in range(2):
        for base, size, axes in PARTS[i]:
            parts[i].append((len(parts[0]) + len(parts[1]), i * SHARE + base, size, axes, at1, at2))
            at1, at2 = at1 + size // 4, at2 + size // 16

    def final(i, base):
        return i * HALF + core * SHARE + base - i * SHARE

    def give_core(i):
        for p, base, size, axes, at1, at2 in parts[i]:
            for r in range(base, base + size, WIDTH):
                block = (r - i * SHARE) // WIDTH
                core_send[r : r + WIDTH] = share_rows(i, 1 - core, block).astype(bf16)
            at = pl.ds(base, size)
            send(core_send.at[at], core_recv.at[at], ring_send.at[p, 0], ring_recv.at[p, 0], chip(coords, 1 - core))

    def step1(i):
        for p, base, size, axes, at1, at2 in parts[i]:
            n = size // 4
            own = [share_rows(i, core, (r - i * SHARE) // WIDTH) for r in range(base, base + size, WIDTH)]
            wait(core_recv.at[pl.ds(base, size)], ring_recv.at[p, 0])
            for k, r in enumerate(range(base, base + size, WIDTH)):
                half[r : r + WIDTH] = (own[k] + core_recv[r : r + WIDTH].astype(f32)).astype(bf16)
            for j in range(1, 4):
                c, device = along(axes[0], j)
                send(half.at[rows_at(base + c * n, n)], recv1.at[j - 1, pl.ds(at1, n)],
                     ring_send.at[p, 1], ring_recv.at[p, 1], device)

    def step2(i):
        for p, base, size, axes, at1, at2 in parts[i]:
            n, m = size // 4, size // 16
            at = pl.ds(at1, n)
            wait(recv1.at[:, at], ring_recv.at[p, 1])
            total1 = half[rows_at(base + coords[axes[0]] * n, n)].astype(f32)
            for j in range(3):
                total1 = total1 + recv1[j, at].astype(f32)
            sum1[at] = total1.astype(bf16)
            for j in range(1, 4):
                c, device = along(axes[1], j)
                send(sum1.at[rows_at(at1 + c * m, m)], recv2.at[j - 1, pl.ds(at2, m)],
                     ring_send.at[p, 2], ring_recv.at[p, 2], device)

    def step3(i):
        for p, base, size, axes, at1, at2 in parts[i]:
            m = size // 16
            at = pl.ds(at2, m)
            wait(recv2.at[:, at], ring_recv.at[p, 2])
            total2 = sum1[rows_at(at1 + coords[axes[1]] * m, m)].astype(f32)
            for j in range(3):
                total2 = total2 + recv2[j, at].astype(f32)
            c3 = coords[axes[2]]
            recv3[c3, at] = total2.astype(bf16)
            for j in range(1, 4):
                _, device = along(axes[2], j)
                send(recv3.at[c3, at], recv3.at[c3, at], ring_send.at[p, 3], ring_recv.at[p, 3], device)

    def step4(i):
        for p, base, size, axes, at1, at2 in parts[i]:
            n, m = size // 4, size // 16
            at = pl.ds(at2, m)
            wait(recv3.at[pl.ds(0, 3), at], ring_recv.at[p, 3])
            total3 = recv3[0, at].astype(f32)
            for j in range(1, 4):
                total3 = total3 + recv3[j, at].astype(f32)
            mine = rows_at(final(i, base) + coords[axes[0]] * n + coords[axes[1]] * m, m)
            summed[mine] = total3.astype(bf16)
            for j in range(1, 4):
                _, device = along(axes[1], j)
                send(summed.at[mine], summed.at[mine], ring_send.at[p, 4], ring_recv.at[p, 4], device)

    def step5(i):
        for p, base, size, axes, at1, at2 in parts[i]:
            n, m = size // 4, size // 16
            wait(summed.at[pl.ds(0, 3 * m)], ring_recv.at[p, 4])
            mine = rows_at(final(i, base) + coords[axes[0]] * n, n)
            for j in range(1, 4):
                _, device = along(axes[0], j)
                send(summed.at[mine], summed.at[mine], ring_send.at[p, 4 + j], ring_recv.at[p, 4 + j], device)
            send(summed.at[mine], summed.at[mine], ring_send.at[p, 8], ring_recv.at[p, 8], chip(coords, 1 - core))

    def step6(i):
        for j in (1, 3, 2):
            for p, base, size, axes, at1, at2 in parts[i]:
                n = size // 4
                wait(summed.at[pl.ds(0, n)], ring_recv.at[p, 4 + j])
                there = rows_at(final(i, base) + lax.rem(coords[axes[0]] + 4 - j, 4) * n, n)
                send(summed.at[there], summed.at[there], ring_send.at[p, 8], ring_recv.at[p, 8], chip(coords, 1 - core))

    def give_back(step, tu, dv):
        send(slots.at[tu * GROUP + dv], returned.at[step], send_sems.at[7], recv_sems.at[7], (tu, dv))

    wait(q_recv, recv_sems.at[5])
    for j in range(QUERY_PEERS - 1):
        grad_q = grad_q + q_recv[j].astype(f32)
    back(0, SCALE * (grad_q * own_inverse - item_unit))
    give_core(0)
    step1(0)
    wait(k_recv, recv_sems.at[6])
    for j in range(ITEM_PEERS - 1):
        grad_k = grad_k + k_recv[j].astype(f32)
    back(1, SCALE * grad_k)
    give_core(1)

    step1(1)

    grad_x = [mm(grad_pre[i], w_in[i], ((1,), (1,))).astype(bf16) for i in range(2)]
    slots[...] = (
        mm(pick_t[...], jnp.concatenate(grad_x, axis=0)).astype(bf16).reshape(SHARDS, CAP, WIDTH)
    )

    def wait_sent(first, last):
        for p, base, size, axes, at1, at2 in parts[0] + parts[1]:
            n, m = size // 4, size // 16
            counts = (size, 3 * n, 3 * m, 3 * m, 3 * m, n, n, n, size)
            for i in range(first, last):
                wait(summed.at[pl.ds(0, counts[i])], ring_send.at[p, i])

    def give_run(run):
        each_ahead(run // 2, give_back, run % 2 * (GROUP // 2), (run % 2 + 1) * (GROUP // 2))

    give_run(0)
    give_run(1)
    returned[0] = slots[me]
    step2(0)
    give_run(2)
    for ref, i in (
        (requests.at[others], 0),
        (rows.at[others], 1),
        (queries.at[pl.ds(0, QUERY_PEERS - 1)], 2),
        (items.at[pl.ds(0, ITEM_PEERS - 1)], 3),
        (part_sums.at[pl.ds(0, QUERY_PEERS - 1)], 4),
        (q_send, 5),
        (k_send, 6),
    ):
        wait(ref, send_sems.at[i])
    step2(1)
    give_run(3)
    step3(0)
    give_run(4)
    step3(1)
    give_run(5)
    step4(0)
    give_run(6)
    step4(1)
    give_run(7)
    step5(0)
    step5(1)
    wait_sent(0, 4)
    step6(0)
    step6(1)
    for p, base, size, axes, at1, at2 in parts[0] + parts[1]:
        i = base // SHARE
        wait(summed.at[pl.ds(0, size)], ring_recv.at[p, 8])
        for c in range(2):
            at = pl.ds(i * HALF + c * SHARE + base - i * SHARE, size)
            stores.append(pltpu.make_async_copy(summed.at[at], summed_out.at[at], store_sems.at[p * 2 + c]))
            stores[-1].start()

    wait(rows.at[others], recv_sems.at[7])
    stores.append(pltpu.make_async_copy(returned, returned_out, store_sems.at[2 * N_PARTS]))
    stores[-1].start()
    wait(slots.at[others], send_sems.at[7])
    wait_sent(4, 9)
    for store in stores:
        store.wait()


def train_step(owner, offset, table, query_in, query_out, item_in, item_out):
    rows1, rows2 = HALF // 4, HALF // 16
    vmem = pl.BlockSpec(memory_space=pltpu.VMEM)
    hbm = pl.BlockSpec(memory_space=pl.ANY)
    V = pltpu.VMEM
    return pl.pallas_call(
        step_kernel,
        out_shape=(
            jax.ShapeDtypeStruct((1, PAIRS), f32),
            jax.ShapeDtypeStruct((SHARDS, 1, SHARDS), jnp.int32),
            jax.ShapeDtypeStruct((SHARDS, CAP, WIDTH), bf16),
            jax.ShapeDtypeStruct((GRAD_ROWS, WIDTH), bf16),
        ),
        in_specs=[vmem, vmem, hbm, hbm, hbm, hbm, hbm],
        out_specs=(vmem, hbm, hbm, hbm),
        scratch_shapes=[
            V((SHARDS, 1, SHARDS), jnp.int32),
            V((SHARDS, CAP, WIDTH), bf16),
            V((GRAD_ROWS, WIDTH), bf16),
            V((ROWS, WIDTH), f32),
            V((2, WIDTH, HIDDEN), bf16),
            V((2, HIDDEN, WIDTH), bf16),
            V((SHARDS, 1, SHARDS), jnp.int32),
            pltpu.SMEM((SHARDS, 1, SHARDS), jnp.int32),
            V((2, CAP, WIDTH), f32),
            V((SHARDS, CAP, WIDTH), bf16),
            V((SHARDS, CAP, WIDTH), bf16),
            V((2 * PAIRS, SHARDS * CAP), bf16),
            V((SHARDS * CAP, 2 * PAIRS), bf16),
            V((2, PAIRS, HIDDEN), f32),
            V((2, PAIRS, HIDDEN), bf16),
            V((2, PAIRS, WIDTH), f32),
            V((2, PAIRS, WIDTH), f32),
            V((QUERY_PEERS, PAIRS, WIDTH), bf16),
            V((ITEM_PEERS, PAIRS, WIDTH), bf16),
            V((BLOCK_K, BLOCK_Q), f32),
            V((BLOCK_K, BLOCK_Q), bf16),
            V((QUERY_PEERS, QUERY_PEERS, PAIRS), f32),
            V((QUERY_PEERS - 1, PAIRS, WIDTH), bf16),
            V((QUERY_PEERS - 1, PAIRS, WIDTH), bf16),
            V((ITEM_PEERS - 1, PAIRS, WIDTH), bf16),
            V((ITEM_PEERS - 1, PAIRS, WIDTH), bf16),
            V((SHARDS, CAP, WIDTH), bf16),
            V((2, PAIRS, WIDTH), bf16),
            V((2, PAIRS, WIDTH), bf16),
            V((2, PAIRS, HIDDEN), bf16),
            V((HALF, WIDTH), bf16),
            V((HALF, WIDTH), bf16),
            V((HALF, WIDTH), bf16),
            V((rows1, WIDTH), bf16),
            V((3, rows1, WIDTH), bf16),
            V((3, rows2, WIDTH), bf16),
            V((4, rows2, WIDTH), bf16),
            pltpu.SemaphoreType.DMA((6,)),
            pltpu.SemaphoreType.DMA((N_TABLE,)),
            pltpu.SemaphoreType.DMA((N_TABLE,)),
            pltpu.SemaphoreType.DMA((8,)),
            pltpu.SemaphoreType.DMA((8,)),
            pltpu.SemaphoreType.DMA((N_PARTS, 9)),
            pltpu.SemaphoreType.DMA((N_PARTS, 9)),
            pltpu.SemaphoreType.DMA((2 * N_PARTS + 2,)),
        ],
        compiler_params=pltpu.CompilerParams(
            collective_id=0, has_side_effects=True, vmem_limit_bytes=56 << 20
        ),
    )(owner, offset, table, query_in, query_out, item_in, item_out)


def update_kernel(
    asked_ref, returned_ref, summed_ref, loss_ref,
    table_grad, q_in, q_out, k_in, k_out, loss_out,
    asked, returned, summed, total, other, wide_in, wide_out, stage, sems,
):
    loads = [
        pltpu.make_async_copy(src, dst, sems.at[i])
        for i, (src, dst) in enumerate(
            [(summed_ref, summed), (asked_ref, asked), (returned_ref, returned)]
        )
    ]
    for load in loads:
        load.start()
    loss_out[...] = loss_ref[...]

    @pl.loop(0, ROWS, step=256)
    def _(r):
        total[pl.ds(r, 256), :] = jnp.zeros((256, WIDTH), f32)
        other[pl.ds(r, 256), :] = jnp.zeros((256, WIDTH), f32)

    loads[0].wait()
    copies = []
    for i, (out_in, out_out) in enumerate(((q_in, q_out), (k_in, k_out))):
        base = i * HALF
        for c in range(0, HIDDEN, WIDTH):
            at = base + c // (2 * WIDTH) * SHARE + c % (2 * WIDTH)
            wide_in[i, :, c : c + WIDTH] = summed[at : at + WIDTH].astype(f32)
            at += 2 * WIDTH
            wide_out[i, c : c + WIDTH] = summed[at : at + WIDTH].astype(f32)
        copies.append(pltpu.make_async_copy(wide_in.at[i], out_in, sems.at[3 + 2 * i]))
        copies.append(pltpu.make_async_copy(wide_out.at[i], out_out, sems.at[4 + 2 * i]))
        copies[-2].start()
        copies[-1].start()
    loads[1].wait()
    loads[2].wait()

    @pl.loop(0, SHARDS, step=2)
    def _(d):
        for u in range(2):
            stage[u] = returned[d + u].astype(f32)
        count = jnp.maximum(asked[d, 0, CAP], asked[d + 1, 0, CAP])
        for first in range(0, CAP, 8):

            @pl.when(count > first)
            def _():
                for slot in range(first, first + 8, 2):
                    for u in range(2):
                        at = pl.ds(asked[d + u, 0, slot], 1)
                        at2 = pl.ds(asked[d + u, 0, slot + 1], 1)
                        total[at, :] += stage[u, slot : slot + 1, :]
                        other[at2, :] += stage[u, slot + 1 : slot + 2, :]

    cut = ROWS // 8
    for r in range(0, ROWS, cut):

        @pl.loop(r, r + cut, step=128)
        def _(q):
            total[pl.ds(q, 128), :] += other[pl.ds(q, 128), :]

        at = pl.ds(r, cut)
        copies.append(pltpu.make_async_copy(total.at[at], table_grad.at[at], sems.at[7 + r // cut]))
        copies[-1].start()
    for copy in copies:
        copy.wait()


def update(asked, returned, summed, loss):
    vmem = pl.BlockSpec(memory_space=pltpu.VMEM)
    hbm = pl.BlockSpec(memory_space=pl.ANY)
    in_shape = jax.ShapeDtypeStruct((WIDTH, HIDDEN), f32)
    out_shape = jax.ShapeDtypeStruct((HIDDEN, WIDTH), f32)
    table_shape = jax.ShapeDtypeStruct((ROWS, WIDTH), f32)
    loss_shape = jax.ShapeDtypeStruct((1, PAIRS), f32)
    return pl.pallas_call(
        update_kernel,
        out_shape=(table_shape, in_shape, out_shape, in_shape, out_shape, loss_shape),
        in_specs=[hbm, hbm, hbm, vmem],
        out_specs=(hbm,) * 5 + (vmem,),
        scratch_shapes=[
            pltpu.SMEM((SHARDS, 1, SHARDS), jnp.int32),
            pltpu.VMEM((SHARDS, CAP, WIDTH), bf16),
            pltpu.VMEM((GRAD_ROWS, WIDTH), bf16),
            pltpu.VMEM((ROWS, WIDTH), f32),
            pltpu.VMEM((ROWS, WIDTH), f32),
            pltpu.VMEM((2, WIDTH, HIDDEN), f32),
            pltpu.VMEM((2, HIDDEN, WIDTH), f32),
            pltpu.VMEM((2, CAP, WIDTH), f32),
            pltpu.SemaphoreType.DMA((15,)),
        ],
        compiler_params=pltpu.CompilerParams(vmem_limit_bytes=56 << 20),
    )(asked, returned, summed, loss)


def local(table, feature_owner, feature_offset, query_in, query_out, item_in, item_out):
    loss, asked, returned, summed = train_step(
        feature_owner.T, feature_offset.T, table, query_in, query_out, item_in, item_out
    )
    table_grad, q_in, q_out, k_in, k_out, loss = update(asked, returned, summed, loss)
    return (loss.reshape(PAIRS), table_grad, q_in, q_out, k_in, k_out)


def solution(mesh):
    in_specs = (
        P(("table", "dp"), None),
        P(("table", "dp"), None),
        P(("table", "dp"), None),
        P(),
        P(),
        P(),
        P(),
    )
    out_specs = (P(("table", "dp")), P(("table", "dp"), None), P(), P(), P(), P())
    return jax.shard_map(local, mesh=mesh, in_specs=in_specs, out_specs=out_specs, check_vma=False)
```
